128 devices in a mesh: feat: 8 (over x, z_hi), hid: 16 (over z_lo, y, core).
Axes of the slice: x: 4, y: 4, z: 4 (z_hi: 2, z_lo: 2; z = z_hi * 2 + z_lo), core: 2. Of those that a mesh axis runs over, the one named last changes fastest.
Arguments:
- tokens: bfloat16 [4096, 12288], P('feat'), may hold values from -6 to 6
- preact: bfloat16 [4096, 24576], P('feat', 'hid'), may hold values from -6 to 6
- grad_hidden: bfloat16 [4096, 24576], P('feat', 'hid'), may hold values from -0.59765625 to 0.59765625
- w_packed: bfloat16 [12288, 8192], P('feat', 'hid'), may hold values from -0.109375 to 0.109375
- block_cols: int32 [96, 64], P('feat', 'hid'), may hold values from 0 to 11, as said below
- block_counts: int32 [96, 16], P('feat', 'hid'), may hold values from 2 to 4, as said below
Outputs:
- grad_input: bfloat16 [4096, 12288], P('feat', 'hid')
- grad_weight: bfloat16 [12288, 8192], P('feat', 'hid')
The draws below stay inside these ranges and needn't reach their ends.
Inputs may be any that keep to these rules, and one draw needn't show every extreme that they name: `block_cols`: within one block row and hidden group, the 4 slots hold distinct block columns; slots at or after the count are dead. `block_counts`: in every hidden group some block row has all 4 slots live.
All inputs are finite; a program needn't handle non-finite values.
Results may differ from the reference program's by a relative error of at most 0.022.
Values may be sent and summed in bfloat16 or wider, within the bound.
A program may use at most 256 MiB of HBM per device.

```python
import jax
import jax.numpy as jnp
from jax import lax

D = 12288
FF = 24576
BLOCK = 128
TOK_DEV = 512
TOKENS = 4096
NBR = 96
SLOTS = 4
N_FEAT = 8
N_HID = 16


def draw_block_cols(key, part):
    key = jax.random.fold_in(key, 11)
    local_cols = FF // BLOCK // N_HID
    scores = jax.random.randint(key, (NBR, N_HID, local_cols), 0, 1 << 20)
    scores = scores * local_cols + jnp.arange(local_cols, dtype=jnp.int32)[None, None, :]
    ranked = jnp.argsort(scores, axis=-1)[:, :, :SLOTS]
    return ranked.reshape(NBR, N_HID * SLOTS).astype(jnp.int32)


def draw_block_counts(key, part):
    key = jax.random.fold_in(key, 23)
    count_key, row_key = jax.random.split(key)
    counts = jax.random.randint(count_key, (NBR, N_HID), SLOTS // 2, SLOTS + 1)
    full_rows = jax.random.randint(row_key, (N_HID,), 0, NBR)
    row_ids = jnp.arange(NBR, dtype=jnp.int32)[:, None]
    return jnp.where(row_ids == full_rows[None, :], SLOTS, counts).astype(jnp.int32)


def level_of(rng, shape, pieces, low, largest):
    loudness, own = 1.0, jax.random.fold_in(rng, 6)
    for dim, parts in pieces:
        draws = jnp.exp(jax.random.uniform(jax.random.fold_in(own, dim), (parts,), jnp.float32, low / len(pieces), largest / len(pieces)))
        loudness = loudness * jnp.repeat(draws, shape[dim] // parts).reshape([-1 if axis == dim else 1 for axis in range(len(shape))])
    return loudness


def bell_draw(rng, extent, scale, reach, pieces=(), kind=jnp.bfloat16):
    result = scale * jax.random.normal(rng, extent, jnp.float32)
    if pieces:
        result = result * level_of(rng, extent, pieces, -0.22, 0.18)
    return jnp.clip(result, -reach, reach).astype(kind)


def setup_inputs(seed: int = 0) -> dict:
    arg_keys = jax.random.split(jax.random.key(seed), 7)
    return {
        "tokens": bell_draw(arg_keys[0], (TOKENS, D), 1.0, 6.0, ((0, 8),)),
        "preact": bell_draw(arg_keys[1], (TOKENS, FF), 1.5, 6.0, ((0, 8), (1, 16))),
        "grad_hidden": bell_draw(arg_keys[2], (TOKENS, FF), 0.1, 0.59765625, ((0, 8), (1, 16))),
        "w_packed": bell_draw(arg_keys[3], (D, N_HID * SLOTS * BLOCK), (D // 4) ** -0.5, 0.109375, ((0, 8), (1, 16))),
        "block_cols": draw_block_cols(jax.random.fold_in(arg_keys[6], 71), 0),
        "block_counts": draw_block_counts(jax.random.fold_in(arg_keys[6], 71), 0),
    }


CUBIC = 0.044715
ROOT = 0.7978845608028654


def gelu_slope(values):
    tangent = jnp.tanh(ROOT * (values + CUBIC * values * values * values))
    return 0.5 * (1.0 + tangent) + 0.5 * values * (1.0 - tangent * tangent) * ROOT * (1.0 + 3.0 * CUBIC * values * values)


def reference(tokens, preact, grad_hidden, w_packed, block_cols, block_counts):
    grad_pre = (grad_hidden.astype(jnp.float32) * gelu_slope(preact.astype(jnp.float32))).astype(jnp.bfloat16)
    grad_blocks = grad_pre.reshape(TOKENS, FF // BLOCK, BLOCK)
    local_cols = FF // BLOCK // N_HID
    group_base = jnp.arange(N_HID, dtype=jnp.int32)[None, :, None] * local_cols
    global_ids = (group_base + block_cols.reshape(NBR, N_HID, SLOTS)).astype(jnp.int32)
    live_mask = (jnp.arange(SLOTS, dtype=jnp.int32)[None, None, :] < block_counts[:, :, None]).astype(jnp.float32)

    def one_row(row_index):
        block_ids = lax.dynamic_index_in_dim(global_ids, row_index, 0, keepdims=False).reshape(-1)
        selected = jnp.take(grad_blocks, block_ids, axis=1).astype(jnp.float32)
        selected = selected.reshape(TOKENS, N_HID, SLOTS, BLOCK)
        row_mask = lax.dynamic_index_in_dim(live_mask, row_index, 0, keepdims=False)
        weight_rows = lax.dynamic_slice_in_dim(w_packed, row_index * BLOCK, BLOCK, 0).astype(jnp.float32)
        weight_rows = weight_rows.reshape(BLOCK, N_HID, SLOTS, BLOCK) * row_mask[None, :, :, None]
        partial_value = jnp.einsum('thsj,ihsj->hti', selected, weight_rows)
        rounded_partial = lax.optimization_barrier(partial_value.astype(jnp.bfloat16)).astype(jnp.float32)
        input_rows = jnp.sum(rounded_partial, axis=0).astype(jnp.bfloat16)
        features = lax.dynamic_slice_in_dim(tokens, row_index * BLOCK, BLOCK, 1).astype(jnp.float32)
        features = features.reshape(N_FEAT, TOK_DEV, BLOCK)
        panel_terms = jnp.einsum('pti,ptkj->pikj', features, selected.reshape(N_FEAT, TOK_DEV, N_HID * SLOTS, BLOCK))
        rounded_terms = lax.optimization_barrier(panel_terms.astype(jnp.bfloat16)).astype(jnp.float32)
        weight_grad = jnp.sum(rounded_terms, axis=0).reshape(BLOCK, N_HID, SLOTS, BLOCK) * row_mask[None, :, :, None]
        return input_rows, weight_grad.reshape(BLOCK, N_HID * SLOTS * BLOCK).astype(jnp.bfloat16)

    input_rows, weight_rows = lax.map(one_row, jnp.arange(NBR, dtype=jnp.int32))
    grad_input = input_rows.transpose(1, 0, 2).reshape(TOKENS, D)
    grad_weight = weight_rows.reshape(D, N_HID * SLOTS * BLOCK)
    return grad_input, grad_weight
```

```python
import functools

import jax
import jax.numpy as jnp
from jax import lax
from jax.experimental import pallas as pl
from jax.experimental.pallas import tpu as pltpu
from jax.sharding import PartitionSpec as P

BLOCK = 128
SLOTS = 4
PANEL = 512
ROWS_DEV = 12
WIDE = ROWS_DEV * BLOCK
HALF = WIDE // 2
COLS = 12
CUBIC = 0.044715
ROOT = 0.7978845608028654
MESH = pl.DeviceIdType.MESH
OWN, RIGHT, LEFT, FAR = 0, 1, 2, 3
X_STEP = (0, 1, 3, 2)
UNITS = (
    (0, OWN), (0, RIGHT), (0, LEFT), (1, OWN), (1, RIGHT), (1, LEFT), (0, FAR), (1, FAR),
)


def gelu_slope(values):
    tangent = jnp.tanh(ROOT * (values + CUBIC * values * values * values))
    return 0.5 * (1.0 + tangent) + 0.5 * values * (1.0 - tangent * tangent) * ROOT * (
        1.0 + 3.0 * CUBIC * values * values
    )


def add_rows(dst, dst_row, dst_cols, terms, rows, step=16):
    def body(i, carry):
        off = i * step
        here = (pl.ds(pl.multiple_of(dst_row + off, 16), step), dst_cols)
        total = dst[here].astype(jnp.float32)
        for ref, row, cols in terms:
            total = total + ref[pl.ds(pl.multiple_of(row + off, 16), step), cols].astype(jnp.float32)
        dst[here] = total.astype(jnp.bfloat16)
        return carry

    lax.fori_loop(0, rows // step, body, 0)


def kernel(
    pat_ref, tokens, preact, grad_hidden, w_hbm,
    gi_ref, gw_ref, tp_ref,
    pat_in, pat_s, w_all, g_own, g_peer, tok_s, part, rb1, r2, rb3, dw, dx,
    send, recv, local,
):
    f, h = lax.axis_index("feat"), lax.axis_index("hid")
    x, zh, zl, y, c = f // 2, f % 2, h // 8, (h // 2) % 4, h % 2

    def dev(x_, zh_, zl_, y_, c_):
        return (x_ * 2 + zh_, zl_ * 8 + y_ * 2 + c_)

    xg = [(x + s) % 4 for s in X_STEP]
    core = dev(x, zh, zl, y, 1 - c)
    xr, xl, xo = dev(xg[RIGHT], zh, zl, y, c), dev(xg[LEFT], zh, zl, y, c), dev(xg[FAR], zh, zl, y, c)
    yr, yl = dev(x, zh, zl, (y + 1) % 4, c), dev(x, zh, zl, (y + 3) % 4, c)
    zlp, zhp = dev(x, zh, 1 - zl, y, c), dev(x, 1 - zh, zl, y, c)

    count = {"remote": 0, "local": 1}
    sends = []

    def remote(src, dst, device):
        i = count["remote"]
        count["remote"] += 1
        cp = pltpu.make_async_remote_copy(
            src_ref=src, dst_ref=dst, send_sem=send.at[i], recv_sem=recv.at[i],
            device_id=device, device_id_type=MESH,
        )
        sends.append(cp)
        return cp

    def near(src, dst):
        i = count["local"]
        count["local"] += 1
        return pltpu.make_async_copy(src, dst, local.at[i])

    pre_in, gh_in = near(preact, part.at[6]), near(grad_hidden, part.at[7])
    w_in = near(w_hbm, w_all.at[OWN])
    pat_own = near(pat_ref, pat_s.at[OWN])
    for cp in (pre_in, gh_in, w_in, pat_own):
        cp.start()

    barrier = pltpu.get_barrier_semaphore()

    def greet(device):
        pl.semaphore_signal(barrier, inc=1, device_id=device, device_id_type=MESH)

    for device in (core, xr, xl, xo, yr, yl, zlp, zhp):
        greet(device)
    mine = (y % 2) == zh
    for other in range(16):
        skip = jnp.logical_and(mine, h == other)

        @pl.when(jnp.logical_not(skip))
        def _():
            greet((x * 2 + y % 2, jnp.int32(other)))

    pl.semaphore_wait(barrier, 24 - mine.astype(jnp.int32))

    pats = [
        remote(pat_ref, pat_in.at[0], xr), remote(pat_ref, pat_in.at[1], xl), remote(pat_ref, pat_in.at[2], xo),
    ]
    w_right = remote(w_hbm, w_all.at[LEFT], xr)
    w_left = remote(w_hbm, w_all.at[RIGHT], xl)
    for cp in pats:
        cp.start()
    w_right.start()
    w_left.start()

    piece = pl.multiple_of(c * 256 + y * 64, 64)
    rows_of = lambda at, n: pl.ds(pl.multiple_of(at, 16), n)

    def group_cols(k, zh_):
        return pl.ds(pl.multiple_of((2 * xg[k] + zh_) * WIDE, 128), WIDE)

    t0 = {
        k: remote(tokens.at[pl.ds(piece, 64), group_cols(k, 1 - zh)], tp_ref.at[k, pl.ds(piece, 64)], zhp)
        for k in range(4)
    }
    t0[FAR].start()
    t0[RIGHT].start()

    pre_in.wait()
    gh_in.wait()

    def slope_step(i, carry):
        rows = pl.ds(pl.multiple_of(i * 16, 16), 16)
        value = part[6, rows, :].astype(jnp.float32)
        grad = (part[7, rows, :].astype(jnp.float32) * gelu_slope(value)).astype(jnp.bfloat16)
        for b in range(COLS):
            g_own[b, rows, :] = grad[:, b * BLOCK:(b + 1) * BLOCK]
        return carry

    lax.fori_loop(0, PANEL // 16, slope_step, 0)
    g_send = remote(g_own, g_peer, zhp)
    g_send.start()
    w_in.wait()
    pat_own.wait()

    def selected(panel, k, r):
        grad = (g_own, g_peer)[panel]
        return jnp.concatenate([grad[pat_s[k, r, s]] for s in range(SLOTS)], axis=1)

    lanes = lambda: lax.broadcasted_iota(jnp.int32, (BLOCK, SLOTS * BLOCK), 1)

    def partial_unit(u):
        panel, k = UNITS[u]

        def body(i, carry):
            for v in range(2):
                r = 2 * i + v
                at = pl.ds(pl.multiple_of(r * BLOCK, BLOCK), BLOCK)
                weights = jnp.where(
                    lanes() < pat_s[k, r, SLOTS] * BLOCK, w_all[k, at, :], jnp.zeros((), jnp.bfloat16)
                )
                part[u, :, at] = lax.dot_general(
                    selected(panel, k, r), weights, (((1,), (1,)), ((), ())),
                    preferred_element_type=jnp.float32,
                ).astype(jnp.bfloat16)
            return carry

        lax.fori_loop(0, ROWS_DEV // 2, body, 0)

    def weight_unit(k, slot):
        def body(r, carry):
            at = pl.ds(pl.multiple_of(r * BLOCK, BLOCK), BLOCK)
            total = 0.0
            for panel in range(2):
                total = total + lax.dot_general(
                    tok_s[slot, panel, :, at], selected(panel, k, r), (((0,), (0,)), ((), ())),
                    preferred_element_type=jnp.float32,
                )
            total = jnp.where(lanes() < pat_s[k, r, SLOTS] * BLOCK, total, 0.0)
            dw[k, at, :] = total.astype(jnp.bfloat16)
            return carry

        lax.fori_loop(0, ROWS_DEV, body, 0)

    A, B = pl.ds(0, HALF), pl.ds(HALF, HALF)
    chunk = lambda t: pl.multiple_of(c * 256 + ((y + t) % 4) * 64, 64)
    stage = {}

    def start_core(u):
        cp = remote(part.at[u, rows_of((1 - c) * 256, 256)], rb1.at[u], core)
        cp.start()
        stage[u, 1] = cp

    def start_ring(u):
        stage[u, 1].wait_recv()
        add_rows(part.at[u], c * 256, slice(None), [(rb1.at[u], 0, slice(None))], 256)
        cps = [
            remote(part.at[u, rows_of(chunk(2), 64), A], r2.at[u, 0], yr),
            remote(part.at[u, rows_of(chunk(2), 64), B], r2.at[u, 1], yl),
            remote(part.at[u, rows_of(chunk(1), 64), B], r2.at[u, 2], yr),
            remote(part.at[u, rows_of(chunk(3), 64), A], r2.at[u, 3], yl),
        ]
        for cp in cps:
            cp.start()
        stage[u, 2] = cps

    def step_ring(u):
        cps = stage[u, 2]
        cps[0].wait_recv()
        add_rows(part.at[u], chunk(1), A, [(r2.at[u, 0], 0, slice(None))], 64)
        right = remote(part.at[u, rows_of(chunk(1), 64), A], r2.at[u, 4], yr)
        right.start()
        cps[1].wait_recv()
        add_rows(part.at[u], chunk(3), B, [(r2.at[u, 1], 0, slice(None))], 64)
        left = remote(part.at[u, rows_of(chunk(3), 64), B], r2.at[u, 5], yl)
        left.start()
        stage[u, 3] = (right, left)

    def end_ring(u):
        stage[u, 2][3].wait_recv()
        stage[u, 3][0].wait_recv()
        every = slice(None)
        add_rows(part.at[u], chunk(0), A, [(r2.at[u, 3], 0, every), (r2.at[u, 4], 0, every)], 64)
        stage[u, 2][2].wait_recv()
        stage[u, 3][1].wait_recv()
        add_rows(part.at[u], chunk(0), B, [(r2.at[u, 2], 0, every), (r2.at[u, 5], 0, every)], 64)
        cp = remote(part.at[u, rows_of(chunk(0) + (1 - zl) * 32, 32)], rb3.at[u], zlp)
        cp.start()
        stage[u, 4] = cp

    finals = []

    def to_owner(u):
        panel, k = UNITS[u]
        stage[u, 4].wait_recv()
        keep = chunk(0) + zl * 32
        add_rows(part.at[u], keep, slice(None), [(rb3.at[u], 0, slice(None))], 32)
        for j, cols in enumerate((A, B)):
            owner_h = 4 * xg[k] + 2 * zh + j
            owner_f = x * 2 + (zh if panel == 0 else 1 - zh)
            src = part.at[u, rows_of(keep, 32), cols]
            dst = gi_ref.at[rows_of(keep, 32)]
            i = count["remote"]
            count["remote"] += 1
            cp = pltpu.make_async_remote_copy(
                src_ref=src, dst_ref=dst, send_sem=send.at[i], recv_sem=local.at[0],
                device_id=(owner_f, owner_h), device_id_type=MESH,
            )
            if panel == 0:
                here = owner_h == h
                stay = pltpu.make_async_copy(src, dst, local.at[0])

                @pl.when(here)
                def _():
                    stay.start()

                @pl.when(jnp.logical_not(here))
                def _():
                    cp.start()
            else:
                here = None
                cp.start()
            finals.append((cp, here))

    t1, t2, t3 = {}, {}, {}

    def tok_spread(k):
        t0[k].wait_recv()
        at = tp_ref.at[k, pl.ds(piece, 64)]
        t1[k] = (remote(at, at, yr), remote(at, at, yl))
        for cp in t1[k]:
            cp.start()

    def tok_forward(k):
        t1[k][0].wait_recv()
        at = tp_ref.at[k, rows_of(chunk(3), 32)]
        right = remote(at, at, yr)
        right.start()
        t1[k][1].wait_recv()
        at = tp_ref.at[k, rows_of(chunk(1) + 32, 32)]
        left = remote(at, at, yl)
        left.start()
        t2[k] = (right, left)

    def tok_core(k):
        for cp in t2[k]:
            cp.wait_recv()
        at = tp_ref.at[k, rows_of(c * 256, 256)]
        t3[k] = remote(at, at, core)
        t3[k].start()

    loads = {}

    def load_own(k, slot):
        loads[k, 0] = near(tokens.at[:, group_cols(k, zh)], tok_s.at[slot, 0])
        loads[k, 0].start()

    def load_peer(k, slot):
        t3[k].wait_recv()
        loads[k, 1] = near(tp_ref.at[k], tok_s.at[slot, 1])
        loads[k, 1].start()

    def weight_group(k, slot):
        loads[k, 0].wait()
        loads[k, 1].wait()
        weight_unit(k, slot)

    partial_unit(0)
    start_core(0)
    load_own(FAR, 0)
    load_own(RIGHT, 1)
    start_ring(0)
    tok_spread(FAR)
    tok_spread(RIGHT)
    step_ring(0)
    tok_forward(FAR)
    end_ring(0)
    tok_forward(RIGHT)
    to_owner(0)
    t0[LEFT].start()
    t0[OWN].start()
    tok_core(FAR)
    tok_core(RIGHT)
    load_peer(FAR, 0)
    load_peer(RIGHT, 1)
    for i, k in ((0, LEFT), (1, RIGHT), (2, FAR)):
        pats[i].wait_recv()
        cp = near(pat_in.at[i], pat_s.at[k])
        cp.start()
        cp.wait()
    w_right.wait_recv()
    w_left.wait_recv()
    top, low = pl.ds(0, HALF), pl.ds(HALF, HALF)
    w_far = (
        remote(w_all.at[LEFT, top], w_all.at[FAR, top], xr),
        remote(w_all.at[RIGHT, low], w_all.at[FAR, low], xl),
    )
    for cp in w_far:
        cp.start()
    partial_unit(1)
    start_core(1)
    partial_unit(2)
    start_core(2)
    start_ring(1)
    tok_spread(LEFT)
    tok_spread(OWN)
    g_send.wait_recv()
    start_ring(2)
    partial_unit(3)
    start_core(3)
    step_ring(1)
    tok_forward(LEFT)
    weight_group(FAR, 0)
    d1 = (remote(dw.at[FAR, top], dx.at[0], xr), remote(dw.at[FAR, low], dx.at[1], xl))
    for cp in d1:
        cp.start()
    load_own(LEFT, 0)
    end_ring(1)
    step_ring(2)
    start_ring(3)
    tok_forward(OWN)
    tok_core(LEFT)
    weight_group(RIGHT, 1)
    load_own(OWN, 1)
    load_peer(LEFT, 0)
    dr = remote(dw.at[RIGHT, low], dx.at[2], xr)
    dr.start()
    to_owner(1)
    end_ring(2)
    step_ring(3)
    partial_unit(4)
    start_core(4)
    tok_core(OWN)
    weight_group(LEFT, 0)
    dl = remote(dw.at[LEFT, top], dx.at[3], xl)
    dl.start()
    load_peer(OWN, 1)
    start_ring(4)
    to_owner(2)
    end_ring(3)
    partial_unit(5)
    start_core(5)
    step_ring(4)
    to_owner(3)
    d1[0].wait_recv()
    add_rows(dw.at[RIGHT], 0, slice(None), [(dx.at[0], 0, slice(None))], HALF)
    d2r = remote(dw.at[RIGHT, top], dx.at[4], xr)
    d2r.start()
    d1[1].wait_recv()
    add_rows(dw.at[LEFT], HALF, slice(None), [(dx.at[1], 0, slice(None))], HALF)
    d2l = remote(dw.at[LEFT, low], dx.at[5], xl)
    d2l.start()
    start_ring(5)
    end_ring(4)
    for cp in w_far:
        cp.wait_recv()
    partial_unit(6)
    start_core(6)
    step_ring(5)
    to_owner(4)
    start_ring(6)
    partial_unit(7)
    start_core(7)
    end_ring(5)
    step_ring(6)
    start_ring(7)
    weight_group(OWN, 1)
    to_owner(5)
    end_ring(6)
    step_ring(7)
    to_owner(6)
    end_ring(7)
    to_owner(7)

    every = slice(None)

    def finish(row, first, second):
        def body(i, carry):
            here = pl.ds(pl.multiple_of(row + i * 16, 16), 16)
            there = pl.ds(pl.multiple_of(i * 16, 16), 16)
            total = dw[OWN, here, :].astype(jnp.float32) + dx[first, there, :].astype(jnp.float32)
            total = total + dx[second, there, :].astype(jnp.float32)
            gw_ref[here, :] = total.astype(jnp.bfloat16)
            return carry

        lax.fori_loop(0, HALF // 16, body, 0)

    dl.wait_recv()
    d2r.wait_recv()
    finish(0, 3, 4)
    dr.wait_recv()
    d2l.wait_recv()
    finish(HALF, 2, 5)
    pltpu.make_async_copy(gi_ref, gi_ref, local.at[0]).wait()

    for cp in sends:
        cp.wait_send()
    for cp, here in finals:
        if here is None:
            cp.wait_send()
        else:

            @pl.when(jnp.logical_not(here))
            def _():
                cp.wait_send()


N_REMOTE = 128
N_LOCAL = 24


def per_device(tokens, preact, grad_hidden, w_packed, block_cols, block_counts):
    pattern = jnp.concatenate([block_cols, block_counts], axis=1)
    pattern = jnp.pad(pattern, ((0, 16 - ROWS_DEV), (0, BLOCK - SLOTS - 1)))
    any_space = pl.BlockSpec(memory_space=pl.ANY)
    vmem = pl.BlockSpec(memory_space=pltpu.VMEM)
    bf16 = jnp.bfloat16
    grad_input, grad_weight, _ = pl.pallas_call(
        kernel,
        out_shape=(
            jax.ShapeDtypeStruct((PANEL, HALF), bf16),
            jax.ShapeDtypeStruct((WIDE, SLOTS * BLOCK), bf16),
            jax.ShapeDtypeStruct((4, PANEL, WIDE), bf16),
        ),
        in_specs=[vmem, any_space, any_space, any_space, any_space],
        out_specs=(any_space, vmem, any_space),
        scratch_shapes=[
            pltpu.VMEM((3, 16, BLOCK), jnp.int32),
            pltpu.SMEM((4, 16, BLOCK), jnp.int32),
            pltpu.VMEM((4, WIDE, SLOTS * BLOCK), bf16),
            pltpu.VMEM((COLS, PANEL, BLOCK), bf16),
            pltpu.VMEM((COLS, PANEL, BLOCK), bf16),
            pltpu.VMEM((2, 2, PANEL, WIDE), bf16),
            pltpu.VMEM((8, PANEL, WIDE), bf16),
            pltpu.VMEM((8, 256, WIDE), bf16),
            pltpu.VMEM((8, 6, 64, HALF), bf16),
            pltpu.VMEM((8, 32, WIDE), bf16),
            pltpu.VMEM((4, WIDE, SLOTS * BLOCK), bf16),
            pltpu.VMEM((6, HALF, SLOTS * BLOCK), bf16),
            pltpu.SemaphoreType.DMA((N_REMOTE,)),
            pltpu.SemaphoreType.DMA((N_REMOTE,)),
            pltpu.SemaphoreType.DMA((N_LOCAL,)),
        ],
        compiler_params=pltpu.CompilerParams(
            collective_id=0, has_side_effects=True, vmem_limit_bytes=60 << 20
        ),
        name="ffn_backward",
    )(pattern, tokens, preact, grad_hidden, w_packed)
    return grad_input, grad_weight


def solution(mesh):
    placed = (
        P("feat", None),
        P("feat", "hid"),
        P("feat", "hid"),
        P("feat", "hid"),
        P("feat", "hid"),
        P("feat", "hid"),
    )
    return jax.shard_map(
        per_device,
        mesh=mesh,
        in_specs=placed,
        out_specs=(P("feat", "hid"), P("feat", "hid")),
        check_vma=False,
    )
```

```python
import functools

import jax
import jax.numpy as jnp
from jax import lax
from jax.experimental import pallas as pl
from jax.experimental.pallas import tpu as pltpu
from jax.sharding import PartitionSpec as P

BLOCK = 128
SLOTS = 4
PANEL = 512
ROWS_DEV = 12
WIDE = ROWS_DEV * BLOCK
HALF = WIDE // 2
COLS = 12
CUBIC = 0.044715
ROOT = 0.7978845608028654
MESH = pl.DeviceIdType.MESH
OWN, RIGHT, LEFT, FAR = 0, 1, 2, 3
X_STEP = (0, 1, 3, 2)
UNITS = (
    (0, OWN), (0, RIGHT), (0, LEFT), (0, FAR), (1, OWN), (1, RIGHT), (1, LEFT), (1, FAR),
)
UNROLL = 6


def gelu_slope(values):
    tangent = jnp.tanh(ROOT * (values + CUBIC * values * values * values))
    return 0.5 * (1.0 + tangent) + 0.5 * values * (1.0 - tangent * tangent) * ROOT * (
        1.0 + 3.0 * CUBIC * values * values
    )


def add_rows(dst, dst_row, dst_cols, terms, rows, step=32):
    def body(i, carry):
        off = i * step
        here = (pl.ds(pl.multiple_of(dst_row + off, 16), step), dst_cols)
        total = dst[here].astype(jnp.float32)
        for ref, row, cols in terms:
            total = total + ref[pl.ds(pl.multiple_of(row + off, 16), step), cols].astype(jnp.float32)
        dst[here] = total.astype(jnp.bfloat16)
        return carry

    lax.fori_loop(0, rows // step, body, 0)


def kernel(
    pat_ref, tokens, preact, grad_hidden, w_hbm,
    gi_ref, gw_ref, tp_ref,
    pat_in, pat_s, w_all, g_own, g_peer, tok_s, part, rb1, r2, rb3, dw, dx,
    send, recv, local,
):
    f, h = lax.axis_index("feat"), lax.axis_index("hid")
    x, zh, zl, y, c = f // 2, f % 2, h // 8, (h // 2) % 4, h % 2

    def dev(x_, zh_, zl_, y_, c_):
        return (x_ * 2 + zh_, zl_ * 8 + y_ * 2 + c_)

    xg = [(x + s) % 4 for s in X_STEP]
    core = dev(x, zh, zl, y, 1 - c)
    xr, xl, xo = dev(xg[RIGHT], zh, zl, y, c), dev(xg[LEFT], zh, zl, y, c), dev(xg[FAR], zh, zl, y, c)
    yr, yl = dev(x, zh, zl, (y + 1) % 4, c), dev(x, zh, zl, (y + 3) % 4, c)
    zlp, zhp = dev(x, zh, 1 - zl, y, c), dev(x, 1 - zh, zl, y, c)

    count = {"remote": 0, "local": 1}
    sends = []
    moving = {}

    def remote(name, src, dst, device):
        i = count["remote"]
        count["remote"] += 1
        cp = pltpu.make_async_remote_copy(
            src_ref=src, dst_ref=dst, send_sem=send.at[i], recv_sem=recv.at[i],
            device_id=device, device_id_type=MESH,
        )
        cp.start()
        sends.append(cp)
        moving[name] = cp.wait_recv

    def near(name, src, dst):
        i = count["local"]
        count["local"] += 1
        cp = pltpu.make_async_copy(src, dst, local.at[i])
        cp.start()
        moving[name] = cp.wait

    def need(*names):
        for name in names:
            wait = moving.get(name)
            if wait is not None:
                wait()
            moving[name] = None

    near("preact", preact, part.at[6])
    near("grad", grad_hidden, part.at[7])
    near(("w", OWN), w_hbm, w_all.at[OWN])
    near(("pat", OWN), pat_ref, pat_s.at[OWN])

    barrier = pltpu.get_barrier_semaphore()

    def greet(device):
        pl.semaphore_signal(barrier, inc=1, device_id=device, device_id_type=MESH)

    for device in (core, xr, xl, xo, yr, yl, zlp, zhp):
        greet(device)
    mine = (y % 2) == zh
    for other in range(8):
        other_y, other_c = other // 2, other % 2
        skip = jnp.logical_and(mine, jnp.logical_and(y == other_y, c == other_c))

        @pl.when(jnp.logical_not(skip))
        def _():
            greet(dev(x, y % 2, zl, other_y, other_c))

    pl.semaphore_wait(barrier, 16 - mine.astype(jnp.int32))

    def start_patterns():
        for i, (k, device) in enumerate(((LEFT, xr), (RIGHT, xl), (FAR, xo))):
            remote(("pat", k), pat_ref, pat_in.at[i], device)

    def start_weights():
        remote(("w", LEFT), w_hbm, w_all.at[LEFT], xr)
        remote(("w", RIGHT), w_hbm, w_all.at[RIGHT], xl)

    def patterns():
        for i, k in enumerate((LEFT, RIGHT, FAR)):
            need(("pat", k))
            near(("pat in", k), pat_in.at[i], pat_s.at[k])
        for k in (LEFT, RIGHT, FAR):
            need(("pat in", k))
        need(("w", OWN), ("pat", OWN))

    top, low = pl.ds(0, HALF), pl.ds(HALF, HALF)

    def forward_weights():
        need(("w", LEFT), ("w", RIGHT))
        remote(("w", FAR), w_all.at[LEFT, top], w_all.at[FAR, top], xr)
        remote("w far low", w_all.at[RIGHT, low], w_all.at[FAR, low], xl)

    piece = pl.multiple_of(c * 256 + y * 64, 64)
    every = slice(None)

    def rows_of(at, n):
        return pl.ds(pl.multiple_of(at, 16), n)

    def group_cols(k, zh_):
        return pl.ds(pl.multiple_of((2 * xg[k] + zh_) * WIDE, 128), WIDE)

    def tok0(k):
        rows = pl.ds(piece, 64)
        remote(("t0", k), tokens.at[rows, group_cols(k, 1 - zh)], tp_ref.at[k, rows], zhp)

    def gelu(half):
        need("preact", "grad")
        cols = pl.ds(half * HALF, HALF)

        def slope_step(i, carry):
            rows = pl.ds(pl.multiple_of(i * 16, 16), 16)
            value = part[6, rows, cols].astype(jnp.float32)
            grad = (part[7, rows, cols].astype(jnp.float32) * gelu_slope(value)).astype(jnp.bfloat16)
            for b in range(COLS // 2):
                g_own[half * COLS // 2 + b, rows, :] = grad[:, b * BLOCK:(b + 1) * BLOCK]
            return carry

        lax.fori_loop(0, PANEL // 16, slope_step, 0)
        blocks = pl.ds(half * COLS // 2, COLS // 2)
        remote(("g", half), g_own.at[blocks], g_peer.at[blocks], zhp)

    def selected(panel, k, r, rows):
        grad = (g_own, g_peer)[panel]
        return jnp.concatenate([grad[pat_s[k, r, s], rows, :] for s in range(SLOTS)], axis=1)

    def live(k, r):
        lanes = lax.broadcasted_iota(jnp.int32, (BLOCK, SLOTS * BLOCK), 1)
        return lanes < pat_s[k, r, SLOTS] * BLOCK

    def each_row(body):
        def several(i, carry):
            for v in range(UNROLL):
                r = UNROLL * i + v
                body(r, pl.ds(pl.multiple_of(r * BLOCK, BLOCK), BLOCK))
            return carry

        lax.fori_loop(0, ROWS_DEV // UNROLL, several, 0)

    def partial_half(u, rows, extra):
        panel, k = UNITS[u]
        if panel == 1:
            need(("g", 0), ("g", 1))
        if k == FAR:
            need(("w", FAR), "w far low")

        def body(r, at):
            weights = jnp.where(live(k, r), w_all[k, at, :], jnp.zeros((), jnp.bfloat16))
            total = lax.dot_general(
                selected(panel, k, r, rows), weights, (((1,), (1,)), ((), ())),
                preferred_element_type=jnp.float32,
            )
            if extra:
                total = total + rb1[u, :, at].astype(jnp.float32)
            part[u, rows, at] = total.astype(jnp.bfloat16)

        each_row(body)

    A, B = pl.ds(0, HALF), pl.ds(HALF, HALF)

    def chunk(t):
        return pl.multiple_of(c * 256 + ((y + t) % 4) * 64, 64)

    def first(u):
        rows = rows_of((1 - c) * 256, 256)
        partial_half(u, rows, False)
        remote(("core", u), part.at[u, rows], rb1.at[u], core)

    def second(u):
        need(("core", u))
        partial_half(u, rows_of(c * 256, 256), True)
        remote(("r0", u), part.at[u, rows_of(chunk(2), 64), A], r2.at[u, 0], yr)
        remote(("r1", u), part.at[u, rows_of(chunk(2), 64), B], r2.at[u, 1], yl)
        remote(("r2", u), part.at[u, rows_of(chunk(1), 64), B], r2.at[u, 2], yr)
        remote(("r3", u), part.at[u, rows_of(chunk(3), 64), A], r2.at[u, 3], yl)

    def step_right(u):
        need(("r0", u))
        add_rows(part.at[u], chunk(1), A, [(r2.at[u, 0], 0, every)], 64)
        remote(("r4", u), part.at[u, rows_of(chunk(1), 64), A], r2.at[u, 4], yr)

    def step_left(u):
        need(("r1", u))
        add_rows(part.at[u], chunk(3), B, [(r2.at[u, 1], 0, every)], 64)
        remote(("r5", u), part.at[u, rows_of(chunk(3), 64), B], r2.at[u, 5], yl)

    finals = []
    crossing = {}

    def end_ring(u):
        need(("r3", u), ("r4", u))
        add_rows(part.at[u], chunk(0), A, [(r2.at[u, 3], 0, every), (r2.at[u, 4], 0, every)], 64)
        need(("r2", u), ("r5", u))
        add_rows(part.at[u], chunk(0), B, [(r2.at[u, 2], 0, every), (r2.at[u, 5], 0, every)], 64)
        stays = xg[UNITS[u][1]] // 2 == zl
        i = count["remote"]
        count["remote"] += 1
        cp = pltpu.make_async_remote_copy(
            src_ref=part.at[u, rows_of(chunk(0), 64)], dst_ref=rb3.at[u],
            send_sem=send.at[i], recv_sem=recv.at[i], device_id=zlp, device_id_type=MESH,
        )

        @pl.when(jnp.logical_not(stays))
        def _():
            cp.start()

        finals.append((cp, jnp.logical_not(stays)))
        crossing[u] = cp, stays


    def to_owner(u):
        panel, k = UNITS[u]
        cp3, stays = crossing[u]

        @pl.when(stays)
        def _():
            cp3.wait_recv()
            add_rows(part.at[u], chunk(0), every, [(rb3.at[u], 0, every)], 64)

        for j, cols in enumerate((A, B)):
            owner = dev(x, zh if panel == 0 else 1 - zh, zl, (xg[k] % 2) * 2 + zh, j)
            src = part.at[u, rows_of(chunk(0), 64), cols]
            dst = gi_ref.at[rows_of(chunk(0), 64)]
            i = count["remote"]
            count["remote"] += 1
            cp = pltpu.make_async_remote_copy(
                src_ref=src, dst_ref=dst, send_sem=send.at[i], recv_sem=local.at[0],
                device_id=owner, device_id_type=MESH,
            )
            away = stays
            if panel == 0:
                here = jnp.logical_and(owner[1] == h, stays)
                away = jnp.logical_and(owner[1] != h, stays)
                stay = pltpu.make_async_copy(src, dst, local.at[0])

                @pl.when(here)
                def _():
                    stay.start()

            @pl.when(away)
            def _():
                cp.start()

            finals.append((cp, away))

    def spread(k):
        need(("t0", k))
        at = tp_ref.at[k, pl.ds(piece, 64)]
        remote(("t1r", k), at, at, yr)
        remote(("t1l", k), at, at, yl)

    def forward_right(k):
        need(("t1r", k))
        at = tp_ref.at[k, rows_of(chunk(3), 32)]
        remote(("t2r", k), at, at, yr)

    def forward_left(k):
        need(("t1l", k))
        at = tp_ref.at[k, rows_of(chunk(1) + 32, 32)]
        remote(("t2l", k), at, at, yl)

    def tok_core(k):
        need(("t2r", k), ("t2l", k))
        at = tp_ref.at[k, rows_of(c * 256, 256)]
        remote(("t3", k), at, at, core)

    def load_own(k):
        near(("lo", k), tokens.at[:, group_cols(k, zh)], tok_s.at[k])

    def load_peer(k):
        need(("t3", k))
        near(("lp", k), tp_ref.at[k], tok_s.at[k])

    def weight_term(k, panel):
        def body(r, at):
            total = lax.dot_general(
                tok_s[k, :, at], selected(panel, k, r, every), (((0,), (0,)), ((), ())),
                preferred_element_type=jnp.float32,
            )
            total = jnp.where(live(k, r), total, 0.0)
            if panel == 1:
                total = total + dw[k, at, :].astype(jnp.float32)
            dw[k, at, :] = total.astype(jnp.bfloat16)

        each_row(body)

    def term_own(k):
        need(("lo", k))
        weight_term(k, 0)

    def term_peer(k):
        need(("lp", k), ("g", 0), ("g", 1))
        weight_term(k, 1)
        if k == FAR:
            remote("d1r", dw.at[FAR, top], dx.at[0], xr)
            remote("d1l", dw.at[FAR, low], dx.at[1], xl)
        if k == RIGHT:
            remote("dr", dw.at[RIGHT, low], dx.at[2], xr)
        if k == LEFT:
            remote("dl", dw.at[LEFT, top], dx.at[3], xl)

    def pass_right():
        need("d1r")
        add_rows(dw.at[RIGHT], 0, every, [(dx.at[0], 0, every)], HALF)
        remote("d2r", dw.at[RIGHT, top], dx.at[4], xr)

    def pass_left():
        need("d1l")
        add_rows(dw.at[LEFT], HALF, every, [(dx.at[1], 0, every)], HALF)
        remote("d2l", dw.at[LEFT, low], dx.at[5], xl)

    def finish(row, first_, second_):
        def body(i, carry):
            here = pl.ds(pl.multiple_of(row + i * 32, 32), 32)
            there = pl.ds(pl.multiple_of(i * 32, 32), 32)
            total = dw[OWN, here, :].astype(jnp.float32) + dx[first_, there, :].astype(jnp.float32)
            total = total + dx[second_, there, :].astype(jnp.float32)
            gw_ref[here, :] = total.astype(jnp.bfloat16)
            return carry

        lax.fori_loop(0, HALF // 32, body, 0)

    start_patterns()
    start_weights()
    tok0(FAR)
    tok0(RIGHT)
    tok0(LEFT)
    tok0(OWN)
    load_own(FAR)
    load_own(RIGHT)
    load_own(LEFT)
    load_own(OWN)
    gelu(0)
    gelu(1)
    patterns()
    spread(FAR)
    first(0)
    term_own(FAR)
    term_own(RIGHT)
    spread(RIGHT)
    second(0)
    forward_right(FAR)
    forward_left(FAR)
    term_own(LEFT)
    term_own(OWN)
    spread(LEFT)
    forward_right(RIGHT)
    forward_left(RIGHT)
    step_right(0)
    step_left(0)
    spread(OWN)
    tok_core(FAR)
    load_peer(FAR)
    forward_weights()
    forward_right(LEFT)
    forward_left(LEFT)
    tok_core(RIGHT)
    end_ring(0)
    load_peer(RIGHT)
    forward_right(OWN)
    forward_left(OWN)
    first(1)
    first(2)
    tok_core(LEFT)
    second(1)
    tok_core(OWN)
    second(2)
    load_peer(LEFT)
    load_peer(OWN)
    step_right(1)
    step_left(1)
    step_right(2)
    step_left(2)
    end_ring(1)
    term_peer(FAR)
    term_peer(RIGHT)
    term_peer(LEFT)
    term_peer(OWN)
    to_owner(0)
    end_ring(2)
    first(3)
    first(4)
    to_owner(1)
    first(5)
    second(3)
    to_owner(2)
    second(4)
    second(5)
    step_right(3)
    step_left(3)
    first(6)
    second(6)
    pass_right()
    pass_left()
    step_right(4)
    step_left(4)
    step_right(5)
    step_left(5)
    end_ring(3)
    first(7)
    step_right(6)
    step_left(6)
    second(7)
    to_owner(3)
    end_ring(4)
    end_ring(5)
    end_ring(6)
    to_owner(4)
    step_right(7)
    step_left(7)
    to_owner(5)
    to_owner(6)
    end_ring(7)
    to_owner(7)
    need("dl", "d2r")
    finish(0, 3, 4)
    need("dr", "d2l")
    finish(HALF, 2, 5)
    need(*moving)
    if any(started is not None for _, started in finals):
        pltpu.make_async_copy(gi_ref, gi_ref, local.at[0]).wait()

    for cp in sends:
        cp.wait_send()
    for cp, started in finals:

        @pl.when(started)
        def _():
            cp.wait_send()


N_REMOTE = 136
N_LOCAL = 24


def per_device(tokens, preact, grad_hidden, w_packed, block_cols, block_counts):
    pattern = jnp.concatenate([block_cols, block_counts], axis=1)
    pattern = jnp.pad(pattern, ((0, 16 - ROWS_DEV), (0, BLOCK - SLOTS - 1)))
    any_space = pl.BlockSpec(memory_space=pl.ANY)
    vmem = pl.BlockSpec(memory_space=pltpu.VMEM)
    bf16 = jnp.bfloat16
    grad_input, grad_weight, _ = pl.pallas_call(
        kernel,
        out_shape=(
            jax.ShapeDtypeStruct((PANEL, HALF), bf16),
            jax.ShapeDtypeStruct((WIDE, SLOTS * BLOCK), bf16),
            jax.ShapeDtypeStruct((4, PANEL, WIDE), bf16),
        ),
        in_specs=[vmem] + [any_space] * 4,
        out_specs=(any_space, vmem, any_space),
        scratch_shapes=[
            pltpu.VMEM((3, 16, BLOCK), jnp.int32),
            pltpu.SMEM((4, 16, BLOCK), jnp.int32),
            pltpu.VMEM((4, WIDE, SLOTS * BLOCK), bf16),
            pltpu.VMEM((COLS, PANEL, BLOCK), bf16),
            pltpu.VMEM((COLS, PANEL, BLOCK), bf16),
            pltpu.VMEM((4, PANEL, WIDE), bf16),
            pltpu.VMEM((8, PANEL, WIDE), bf16),
            pltpu.VMEM((8, 256, WIDE), bf16),
            pltpu.VMEM((8, 6, 64, HALF), bf16),
            pltpu.VMEM((8, 64, WIDE), bf16),
            pltpu.VMEM((4, WIDE, SLOTS * BLOCK), bf16),
            pltpu.VMEM((6, HALF, SLOTS * BLOCK), bf16),
            pltpu.SemaphoreType.DMA((N_REMOTE,)),
            pltpu.SemaphoreType.DMA((N_REMOTE,)),
            pltpu.SemaphoreType.DMA((N_LOCAL,)),
        ],
        compiler_params=pltpu.CompilerParams(
            collective_id=0, has_side_effects=True, vmem_limit_bytes=60 << 20
        ),
        name="ffn_backward",
    )(pattern, tokens, preact, grad_hidden, w_packed)
    return grad_input, grad_weight


def solution(mesh):
    placed = (
        P("feat", None),
        P("feat", "hid"),
        P("feat", "hid"),
        P("feat", "hid"),
        P("feat", "hid"),
        P("feat", "hid"),
    )
    return jax.shard_map(
        per_device,
        mesh=mesh,
        in_specs=placed,
        out_specs=(P("feat", "hid"), P("feat", "hid")),
        check_vma=False,
    )
```

```python
import functools

import jax
import jax.numpy as jnp
from jax import lax
from jax.experimental import pallas as pl
from jax.experimental.pallas import tpu as pltpu
from jax.sharding import PartitionSpec as P

BLOCK = 128
SLOTS = 4
PANEL = 512
ROWS_DEV = 12
WIDE = ROWS_DEV * BLOCK
HALF = WIDE // 2
COLS = 12
CUBIC = 0.044715
ROOT = 0.7978845608028654
MESH = pl.DeviceIdType.MESH
OWN, RIGHT, LEFT, FAR = 0, 1, 2, 3
X_STEP = (0, 1, 3, 2)
UNITS = (
    (0, OWN), (0, RIGHT), (0, LEFT), (0, FAR), (1, OWN), (1, RIGHT), (1, LEFT), (1, FAR),
)
UNROLL = 6


def gelu_slope(values):
    tangent = jnp.tanh(ROOT * (values + CUBIC * values * values * values))
    return 0.5 * (1.0 + tangent) + 0.5 * values * (1.0 - tangent * tangent) * ROOT * (
        1.0 + 3.0 * CUBIC * values * values
    )


def add_rows(dst, dst_row, dst_cols, terms, rows, step=32):
    def body(i, carry):
        off = i * step
        here = (pl.ds(pl.multiple_of(dst_row + off, 16), step), dst_cols)
        total = dst[here].astype(jnp.float32)
        for ref, row, cols in terms:
            total = total + ref[pl.ds(pl.multiple_of(row + off, 16), step), cols].astype(jnp.float32)
        dst[here] = total.astype(jnp.bfloat16)
        return carry

    lax.fori_loop(0, rows // step, body, 0)


def kernel(
    pat_ref, tokens, preact, grad_hidden, w_hbm,
    gi_ref, gw_ref, tp_ref,
    pat_in, pat_s, w_all, g_own, g_peer, tok_s, part, rb1, r2, rb3, dw, dx,
    send, recv, local,
):
    f, h = lax.axis_index("feat"), lax.axis_index("hid")
    x, zh, zl, y, c = f // 2, f % 2, h // 8, (h // 2) % 4, h % 2

    def dev(x_, zh_, zl_, y_, c_):
        return (x_ * 2 + zh_, zl_ * 8 + y_ * 2 + c_)

    xg = [(x + s) % 4 for s in X_STEP]
    core = dev(x, zh, zl, y, 1 - c)
    xr, xl, xo = dev(xg[RIGHT], zh, zl, y, c), dev(xg[LEFT], zh, zl, y, c), dev(xg[FAR], zh, zl, y, c)
    yr, yl = dev(x, zh, zl, (y + 1) % 4, c), dev(x, zh, zl, (y + 3) % 4, c)
    zlp, zhp = dev(x, zh, 1 - zl, y, c), dev(x, 1 - zh, zl, y, c)

    count = {"remote": 0, "local": 1}
    sends = []
    moving = {}

    def remote(name, src, dst, device):
        i = count["remote"]
        count["remote"] += 1
        cp = pltpu.make_async_remote_copy(
            src_ref=src, dst_ref=dst, send_sem=send.at[i], recv_sem=recv.at[i],
            device_id=device, device_id_type=MESH,
        )
        cp.start()
        sends.append(cp)
        moving[name] = cp.wait_recv

    def near(name, src, dst):
        i = count["local"]
        count["local"] += 1
        cp = pltpu.make_async_copy(src, dst, local.at[i])
        cp.start()
        moving[name] = cp.wait

    def need(*names):
        for name in names:
            wait = moving.get(name)
            if wait is not None:
                wait()
            moving[name] = None

    near("preact", preact, part.at[6])
    near("grad", grad_hidden, part.at[7])
    near(("w", OWN), w_hbm, w_all.at[OWN])
    near(("pat", OWN), pat_ref, pat_s.at[OWN])

    barrier = pltpu.get_barrier_semaphore()

    def greet(device):
        pl.semaphore_signal(barrier, inc=1, device_id=device, device_id_type=MESH)

    for device in (core, xr, xl, xo, yr, yl, zlp, zhp):
        greet(device)
    mine = (y % 2) == zh
    side = jnp.where(c == zl, y, (y + 3 + 2 * zl) % 4)
    for t in range(4):
        for other_c in range(2):
            if t == 0:
                sends_here = jnp.logical_not(jnp.logical_and(mine, c == other_c))
                other_y = jnp.where(mine, y, side)
            else:
                sends_here, other_y = mine, (y + t) % 4

            @pl.when(sends_here)
            def _():
                greet(dev(x, y % 2, zl, other_y, other_c))

    pl.semaphore_wait(barrier, 13 - mine.astype(jnp.int32))

    def start_patterns():
        for i, (k, device) in enumerate(((LEFT, xr), (RIGHT, xl), (FAR, xo))):
            remote(("pat", k), pat_ref, pat_in.at[i], device)

    def start_weights():
        remote(("w", LEFT), w_hbm, w_all.at[LEFT], xr)
        remote(("w", RIGHT), w_hbm, w_all.at[RIGHT], xl)

    def patterns():
        for i, k in enumerate((LEFT, RIGHT, FAR)):
            need(("pat", k))
            near(("pat in", k), pat_in.at[i], pat_s.at[k])
        for k in (LEFT, RIGHT, FAR):
            need(("pat in", k))
        need(("w", OWN), ("pat", OWN))

    top, low = pl.ds(0, HALF), pl.ds(HALF, HALF)

    def forward_weights():
        need(("w", LEFT), ("w", RIGHT))
        remote(("w", FAR), w_all.at[LEFT, top], w_all.at[FAR, top], xr)
        remote("w far low", w_all.at[RIGHT, low], w_all.at[FAR, low], xl)

    piece = pl.multiple_of(c * 256 + y * 64, 64)
    every = slice(None)

    def rows_of(at, n):
        return pl.ds(pl.multiple_of(at, 16), n)

    def group_cols(k, zh_):
        return pl.ds(pl.multiple_of((2 * xg[k] + zh_) * WIDE, 128), WIDE)

    def tok0(k):
        rows = pl.ds(piece, 64)
        remote(("t0", k), tokens.at[rows, group_cols(k, 1 - zh)], tp_ref.at[k, rows], zhp)

    def gelu(half):
        need("preact", "grad")
        cols = pl.ds(half * HALF, HALF)

        def slope_step(i, carry):
            rows = pl.ds(pl.multiple_of(i * 16, 16), 16)
            value = part[6, rows, cols].astype(jnp.float32)
            grad = (part[7, rows, cols].astype(jnp.float32) * gelu_slope(value)).astype(jnp.bfloat16)
            for b in range(COLS // 2):
                g_own[half * COLS // 2 + b, rows, :] = grad[:, b * BLOCK:(b + 1) * BLOCK]
            return carry

        lax.fori_loop(0, PANEL // 16, slope_step, 0)
        blocks = pl.ds(half * COLS // 2, COLS // 2)
        remote(("g", half), g_own.at[blocks], g_peer.at[blocks], zhp)

    def selected(panel, k, r, rows):
        grad = (g_own, g_peer)[panel]
        return jnp.concatenate([grad[pat_s[k, r, s], rows, :] for s in range(SLOTS)], axis=1)

    def live(k, r):
        lanes = lax.broadcasted_iota(jnp.int32, (BLOCK, SLOTS * BLOCK), 1)
        return lanes < pat_s[k, r, SLOTS] * BLOCK

    def each_row(body):
        def several(i, carry):
            for v in range(UNROLL):
                r = UNROLL * i + v
                body(r, pl.ds(pl.multiple_of(r * BLOCK, BLOCK), BLOCK))
            return carry

        lax.fori_loop(0, ROWS_DEV // UNROLL, several, 0)

    def partial_half(u, rows, extra):
        panel, k = UNITS[u]
        if panel == 1:
            need(("g", 0), ("g", 1))
        if k == FAR:
            need(("w", FAR), "w far low")

        def body(r, at):
            weights = jnp.where(live(k, r), w_all[k, at, :], jnp.zeros((), jnp.bfloat16))
            total = lax.dot_general(
                selected(panel, k, r, rows), weights, (((1,), (1,)), ((), ())),
                preferred_element_type=jnp.float32,
            )
            if extra:
                total = total + rb1[u, :, at].astype(jnp.float32)
            part[u, rows, at] = total.astype(jnp.bfloat16)

        each_row(body)

    A, B = pl.ds(0, HALF), pl.ds(HALF, HALF)

    def chunk(t):
        return pl.multiple_of(c * 256 + ((y + t) % 4) * 64, 64)

    def first(u):
        rows = rows_of((1 - c) * 256, 256)
        partial_half(u, rows, False)
        remote(("core", u), part.at[u, rows], rb1.at[u], core)

    def second(u):
        need(("core", u))
        partial_half(u, rows_of(c * 256, 256), True)
        if u < 4:
            ring(u)

    def share(u, t, half):
        if u < 4:
            return part.at[u], chunk(t)
        turn = (y + t - zh) % 4
        group = jnp.where(
            half == 0, (turn % 2) * 2 + turn // 2,
            jnp.where(turn % 2 == 0, 2 + turn // 2, 1 - turn // 2),
        )
        step = (group - x) % 4
        index = jnp.where(step == 2, FAR, jnp.where(step == 3, LEFT, step))
        return part.at[4 + index], pl.multiple_of(c * 256 + (u - 4) * 64, 64)

    def share_at(u, t, half):
        ref, row = share(u, t, half)
        return ref.at[pl.ds(row, 64), pl.ds(pl.multiple_of(half * HALF, 128), HALF)]

    def ring(u):
        remote(("r0", u), share_at(u, 2, 0), r2.at[u, 0], yr)
        remote(("r1", u), share_at(u, 2, 1), r2.at[u, 1], yl)
        remote(("r2", u), share_at(u, 1, 1), r2.at[u, 2], yr)
        remote(("r3", u), share_at(u, 3, 0), r2.at[u, 3], yl)

    def step_right(u):
        need(("r0", u))
        ref, row = share(u, 1, 0)
        add_rows(ref, row, A, [(r2.at[u, 0], 0, every)], 64)
        remote(("r4", u), share_at(u, 1, 0), r2.at[u, 4], yr)

    def step_left(u):
        need(("r1", u))
        ref, row = share(u, 3, 1)
        add_rows(ref, row, B, [(r2.at[u, 1], 0, every)], 64)
        remote(("r5", u), share_at(u, 3, 1), r2.at[u, 5], yl)

    finals = []
    crossing = {}
    odd = (y - zh) % 2
    kept = (odd + zl) % 2

    def end_ring(u):
        need(("r3", u), ("r4", u))
        ref, row = share(u, 0, 0)
        add_rows(ref, row, A, [(r2.at[u, 3], 0, every), (r2.at[u, 4], 0, every)], 64)
        need(("r2", u), ("r5", u))
        ref, row = share(u, 0, 1)
        add_rows(ref, row, B, [(r2.at[u, 2], 0, every), (r2.at[u, 5], 0, every)], 64)
        if u >= 4:
            remote(("zl", u), share_at(u, 0, 1 - kept), rb3.at[u, :, A], zlp)
            return
        stays = xg[UNITS[u][1]] // 2 == zl
        i = count["remote"]
        count["remote"] += 1
        cp = pltpu.make_async_remote_copy(
            src_ref=part.at[u, pl.ds(chunk(0), 64)], dst_ref=rb3.at[u],
            send_sem=send.at[i], recv_sem=recv.at[i], device_id=zlp, device_id_type=MESH,
        )

        @pl.when(jnp.logical_not(stays))
        def _():
            cp.start()

        finals.append((cp, jnp.logical_not(stays)))
        crossing[u] = cp, stays


    def to_owner(u):
        panel, k = UNITS[u]
        if panel == 1:
            need(("zl", u))
            ref, row = share(u, 0, kept)
            cols = pl.ds(pl.multiple_of(kept * HALF, 128), HALF)
            add_rows(ref, row, cols, [(rb3.at[u], 0, A)], 64)
            i = count["remote"]
            count["remote"] += 1
            cp = pltpu.make_async_remote_copy(
                src_ref=share_at(u, 0, kept), dst_ref=gi_ref.at[pl.ds(row, 64)],
                send_sem=send.at[i], recv_sem=local.at[0],
                device_id=dev(x, 1 - zh, zl, (y + 4 + odd * (2 * kept - 1)) % 4, kept),
                device_id_type=MESH,
            )
            cp.start()
            sends.append(cp)
            return
        cp3, stays = crossing[u]

        @pl.when(stays)
        def _():
            cp3.wait_recv()
            add_rows(part.at[u], chunk(0), every, [(rb3.at[u], 0, every)], 64)

        for j, cols in enumerate((A, B)):
            owner = dev(x, zh, zl, (xg[k] % 2) * 2 + zh, j)
            src = part.at[u, pl.ds(chunk(0), 64), cols]
            dst = gi_ref.at[pl.ds(chunk(0), 64)]
            i = count["remote"]
            count["remote"] += 1
            cp = pltpu.make_async_remote_copy(
                src_ref=src, dst_ref=dst, send_sem=send.at[i], recv_sem=local.at[0],
                device_id=owner, device_id_type=MESH,
            )
            here = jnp.logical_and(owner[1] == h, stays)
            away = jnp.logical_and(owner[1] != h, stays)
            stay = pltpu.make_async_copy(src, dst, local.at[0])

            @pl.when(here)
            def _():
                stay.start()

            @pl.when(away)
            def _():
                cp.start()

            finals.append((cp, away))

    def spread(k):
        need(("t0", k))
        at = tp_ref.at[k, pl.ds(piece, 64)]
        remote(("t1r", k), at, at, yr)
        remote(("t1l", k), at, at, yl)

    def forward_right(k):
        need(("t1r", k))
        at = tp_ref.at[k, rows_of(chunk(3), 32)]
        remote(("t2r", k), at, at, yr)

    def forward_left(k):
        need(("t1l", k))
        at = tp_ref.at[k, rows_of(chunk(1) + 32, 32)]
        remote(("t2l", k), at, at, yl)

    def tok_core(k):
        need(("t2r", k), ("t2l", k))
        at = tp_ref.at[k, rows_of(c * 256, 256)]
        remote(("t3", k), at, at, core)

    def load_own(k):
        near(("lo", k), tokens.at[:, group_cols(k, zh)], tok_s.at[k])

    def load_peer(k):
        need(("t3", k))
        near(("lp", k), tp_ref.at[k], tok_s.at[k])

    def weight_term(k, panel):
        def body(r, at):
            total = lax.dot_general(
                tok_s[k, :, at], selected(panel, k, r, every), (((0,), (0,)), ((), ())),
                preferred_element_type=jnp.float32,
            )
            total = jnp.where(live(k, r), total, 0.0)
            if panel == 1:
                total = total + dw[k, at, :].astype(jnp.float32)
            dw[k, at, :] = total.astype(jnp.bfloat16)

        each_row(body)

    def term_own(k):
        need(("lo", k))
        weight_term(k, 0)

    def term_peer(k):
        need(("lp", k), ("g", 0), ("g", 1))
        weight_term(k, 1)
        if k == FAR:
            remote("d1r", dw.at[FAR, top], dx.at[0], xr)
            remote("d1l", dw.at[FAR, low], dx.at[1], xl)
        if k == RIGHT:
            remote("dr", dw.at[RIGHT, low], dx.at[2], xr)
        if k == LEFT:
            remote("dl", dw.at[LEFT, top], dx.at[3], xl)

    def pass_right():
        need("d1r")
        add_rows(dw.at[RIGHT], 0, every, [(dx.at[0], 0, every)], HALF)
        remote("d2r", dw.at[RIGHT, top], dx.at[4], xr)

    def pass_left():
        need("d1l")
        add_rows(dw.at[LEFT], HALF, every, [(dx.at[1], 0, every)], HALF)
        remote("d2l", dw.at[LEFT, low], dx.at[5], xl)

    def finish(row, first_, second_):
        def body(i, carry):
            here = pl.ds(pl.multiple_of(row + i * 32, 32), 32)
            there = pl.ds(pl.multiple_of(i * 32, 32), 32)
            total = dw[OWN, here, :].astype(jnp.float32) + dx[first_, there, :].astype(jnp.float32)
            total = total + dx[second_, there, :].astype(jnp.float32)
            gw_ref[here, :] = total.astype(jnp.bfloat16)
            return carry

        lax.fori_loop(0, HALF // 32, body, 0)

    start_patterns()
    start_weights()
    tok0(FAR)
    tok0(RIGHT)
    tok0(LEFT)
    tok0(OWN)
    load_own(FAR)
    load_own(RIGHT)
    load_own(LEFT)
    load_own(OWN)
    gelu(0)
    gelu(1)
    patterns()
    first(0)
    spread(FAR)
    term_own(FAR)
    term_own(RIGHT)
    term_own(LEFT)
    spread(RIGHT)
    second(0)
    term_own(OWN)
    forward_right(FAR)
    forward_left(FAR)
    spread(LEFT)
    forward_right(RIGHT)
    forward_left(RIGHT)
    spread(OWN)
    step_right(0)
    step_left(0)
    tok_core(FAR)
    load_peer(FAR)
    forward_right(LEFT)
    forward_left(LEFT)
    tok_core(RIGHT)
    load_peer(RIGHT)
    forward_weights()
    forward_right(OWN)
    forward_left(OWN)
    first(1)
    end_ring(0)
    tok_core(LEFT)
    second(1)
    tok_core(OWN)
    first(2)
    load_peer(LEFT)
    load_peer(OWN)
    step_right(1)
    step_left(1)
    second(2)
    end_ring(1)
    step_right(2)
    step_left(2)
    term_peer(FAR)
    term_peer(RIGHT)
    first(3)
    end_ring(2)
    first(4)
    second(3)
    first(5)
    first(6)
    second(4)
    first(7)
    second(5)
    second(6)
    step_right(3)
    step_left(3)
    second(7)
    ring(4)
    ring(5)
    term_peer(LEFT)
    step_right(4)
    step_left(4)
    ring(6)
    pass_right()
    pass_left()
    step_right(5)
    step_left(5)
    ring(7)
    term_peer(OWN)
    end_ring(3)
    end_ring(4)
    step_right(6)
    step_left(6)
    end_ring(5)
    step_right(7)
    step_left(7)
    end_ring(6)
    to_owner(4)
    to_owner(5)
    end_ring(7)
    to_owner(0)
    to_owner(1)
    to_owner(2)
    to_owner(3)
    to_owner(6)
    to_owner(7)
    need("dl", "d2r")
    finish(0, 3, 4)
    need("dr", "d2l")
    finish(HALF, 2, 5)
    need(*moving)
    if finals:
        pltpu.make_async_copy(gi_ref, gi_ref, local.at[0]).wait()

    for cp in sends:
        cp.wait_send()
    for cp, started in finals:

        @pl.when(started)
        def _():
            cp.wait_send()


N_REMOTE = 136
N_LOCAL = 24


def per_device(tokens, preact, grad_hidden, w_packed, block_cols, block_counts):
    pattern = jnp.concatenate([block_cols, block_counts], axis=1)
    pattern = jnp.pad(pattern, ((0, 16 - ROWS_DEV), (0, BLOCK - SLOTS - 1)))
    any_space = pl.BlockSpec(memory_space=pl.ANY)
    vmem = pl.BlockSpec(memory_space=pltpu.VMEM)
    bf16 = jnp.bfloat16
    grad_input, grad_weight, _ = pl.pallas_call(
        kernel,
        out_shape=(
            jax.ShapeDtypeStruct((PANEL, HALF), bf16),
            jax.ShapeDtypeStruct((WIDE, SLOTS * BLOCK), bf16),
            jax.ShapeDtypeStruct((4, PANEL, WIDE), bf16),
        ),
        in_specs=[vmem] + [any_space] * 4,
        out_specs=(any_space, vmem, any_space),
        scratch_shapes=[
            pltpu.VMEM((3, 16, BLOCK), jnp.int32),
            pltpu.SMEM((4, 16, BLOCK), jnp.int32),
            pltpu.VMEM((4, WIDE, SLOTS * BLOCK), bf16),
            pltpu.VMEM((COLS, PANEL, BLOCK), bf16),
            pltpu.VMEM((COLS, PANEL, BLOCK), bf16),
            pltpu.VMEM((4, PANEL, WIDE), bf16),
            pltpu.VMEM((8, PANEL, WIDE), bf16),
            pltpu.VMEM((8, 256, WIDE), bf16),
            pltpu.VMEM((8, 6, 64, HALF), bf16),
            pltpu.VMEM((8, 64, WIDE), bf16),
            pltpu.VMEM((4, WIDE, SLOTS * BLOCK), bf16),
            pltpu.VMEM((6, HALF, SLOTS * BLOCK), bf16),
            pltpu.SemaphoreType.DMA((N_REMOTE,)),
            pltpu.SemaphoreType.DMA((N_REMOTE,)),
            pltpu.SemaphoreType.DMA((N_LOCAL,)),
        ],
        compiler_params=pltpu.CompilerParams(
            collective_id=0, has_side_effects=True, vmem_limit_bytes=60 << 20
        ),
        name="ffn_backward",
    )(pattern, tokens, preact, grad_hidden, w_packed)
    return grad_input, grad_weight


def solution(mesh):
    placed = (
        P("feat", None),
        P("feat", "hid"),
        P("feat", "hid"),
        P("feat", "hid"),
        P("feat", "hid"),
        P("feat", "hid"),
    )
    return jax.shard_map(
        per_device,
        mesh=mesh,
        in_specs=placed,
        out_specs=(P("feat", "hid"), P("feat", "hid")),
        check_vma=False,
    )
```

```python
import functools

import jax
import jax.numpy as jnp
from jax import lax
from jax.experimental import pallas as pl
from jax.experimental.pallas import tpu as pltpu
from jax.sharding import PartitionSpec as P

BLOCK = 128
SLOTS = 4
PANEL = 512
ROWS_DEV = 12
WIDE = ROWS_DEV * BLOCK
HALF = WIDE // 2
COLS = 12
CUBIC = 0.044715
ROOT = 0.7978845608028654
MESH = pl.DeviceIdType.MESH
OWN, RIGHT, LEFT, FAR = 0, 1, 2, 3
X_STEP = (0, 1, 3, 2)
UNITS = (
    (0, OWN), (0, RIGHT), (0, LEFT), (0, FAR), (1, OWN), (1, RIGHT), (1, LEFT), (1, FAR),
)
UNROLL = 6


def gelu_slope(values):
    tangent = jnp.tanh(ROOT * (values + CUBIC * values * values * values))
    return 0.5 * (1.0 + tangent) + 0.5 * values * (1.0 - tangent * tangent) * ROOT * (
        1.0 + 3.0 * CUBIC * values * values
    )


def add_rows(dst, dst_row, dst_cols, terms, rows, step=32):
    def body(i, carry):
        off = i * step
        here = (pl.ds(pl.multiple_of(dst_row + off, 16), step), dst_cols)
        total = dst[here].astype(jnp.float32)
        for ref, row, cols in terms:
            total = total + ref[pl.ds(pl.multiple_of(row + off, 16), step), cols].astype(jnp.float32)
        dst[here] = total.astype(jnp.bfloat16)
        return carry

    lax.fori_loop(0, rows // step, body, 0)


def kernel(
    cols_ref, counts_ref, tokens, preact, grad_hidden, w_hbm,
    gi_ref, gw_ref, tp_ref,
    pat_ref, pat_in, pat_s, w_all, g_own, g_peer, tok_s, part, rb1, r2, rb3, rb4, dw, dx,
    send, recv, local,
):
    f, h = lax.axis_index("feat"), lax.axis_index("hid")
    x, zh, zl, y, c = f // 2, f % 2, h // 8, (h // 2) % 4, h % 2

    def dev(x_, zh_, zl_, y_, c_):
        return (x_ * 2 + zh_, zl_ * 8 + y_ * 2 + c_)

    xg = [(x + s) % 4 for s in X_STEP]
    core = dev(x, zh, zl, y, 1 - c)
    xr, xl, xo = dev(xg[RIGHT], zh, zl, y, c), dev(xg[LEFT], zh, zl, y, c), dev(xg[FAR], zh, zl, y, c)
    yr, yl = dev(x, zh, zl, (y + 1) % 4, c), dev(x, zh, zl, (y + 3) % 4, c)
    zlp, zhp = dev(x, zh, 1 - zl, y, c), dev(x, 1 - zh, zl, y, c)

    count = {"remote": 0, "local": 1}
    sends = []
    moving = {}

    def remote(name, src, dst, device):
        i = count["remote"]
        count["remote"] += 1
        cp = pltpu.make_async_remote_copy(
            src_ref=src, dst_ref=dst, send_sem=send.at[i], recv_sem=recv.at[i],
            device_id=device, device_id_type=MESH,
        )
        cp.start()
        sends.append(cp)
        moving[name] = cp.wait_recv

    def near(name, src, dst):
        i = count["local"]
        count["local"] += 1
        cp = pltpu.make_async_copy(src, dst, local.at[i])
        cp.start()
        moving[name] = cp.wait

    def need(*names):
        for name in names:
            wait = moving.get(name)
            if wait is not None:
                wait()
            moving[name] = None

    near("preact", preact, part.at[6])
    near("grad", grad_hidden, part.at[7])
    near(("w", OWN), w_hbm, w_all.at[OWN])
    pat_ref[...] = jnp.zeros_like(pat_ref)
    pat_ref[:SLOTS, :ROWS_DEV] = cols_ref[...]
    pat_ref[SLOTS:SLOTS + 1, :ROWS_DEV] = counts_ref[...]
    near(("pat", OWN), pat_ref, pat_s.at[OWN])

    barrier = pltpu.get_barrier_semaphore()

    def greet(device):
        pl.semaphore_signal(barrier, inc=1, device_id=device, device_id_type=MESH)

    for device in (core, xr, xl, xo, yr, yl, zlp, zhp):
        greet(device)
    mine = (y % 2) == zh
    side = jnp.where(c == zl, y, (y + 3 + 2 * zl) % 4)
    for t in range(4):
        for other_c in range(2):
            other_y = (y + t) % 4
            if t == 0:
                other_y = jnp.where(mine, y, side)
                sends_here = jnp.logical_not(jnp.logical_and(other_y == y, c == other_c))
            else:
                sends_here = mine

            @pl.when(sends_here)
            def _():
                greet(dev(x, zh, zl, other_y, other_c))

    stay_put = jnp.logical_and(jnp.logical_not(mine), c == zl)
    pl.semaphore_wait(barrier, 13 - mine.astype(jnp.int32) - stay_put.astype(jnp.int32))

    def start_patterns():
        for i, (k, device) in enumerate(((LEFT, xr), (RIGHT, xl), (FAR, xo))):
            remote(("pat", k), pat_ref, pat_in.at[i], device)

    def start_weights():
        remote(("w", LEFT), w_hbm, w_all.at[LEFT], xr)
        remote(("w", RIGHT), w_hbm, w_all.at[RIGHT], xl)

    def patterns():
        for i, k in enumerate((LEFT, RIGHT, FAR)):
            need(("pat", k))
            near(("pat in", k), pat_in.at[i], pat_s.at[k])
        for k in (LEFT, RIGHT, FAR):
            need(("pat in", k))
        need(("w", OWN), ("pat", OWN))

    top, low = pl.ds(0, HALF), pl.ds(HALF, HALF)

    def forward_weights():
        need(("w", LEFT), ("w", RIGHT))
        remote(("w", FAR), w_all.at[LEFT, top], w_all.at[FAR, top], xr)
        remote("w far low", w_all.at[RIGHT, low], w_all.at[FAR, low], xl)

    piece = pl.multiple_of(c * 256 + y * 64, 64)
    every = slice(None)

    def rows_of(at, n):
        return pl.ds(pl.multiple_of(at, 16), n)

    def group_cols(k, zh_):
        return pl.ds(pl.multiple_of((2 * xg[k] + zh_) * WIDE, 128), WIDE)

    def tok0(k):
        rows = pl.ds(piece, 64)
        remote(("t0", k), tokens.at[rows, group_cols(k, 1 - zh)], tp_ref.at[k, rows], zhp)

    def gelu(half):
        need("preact", "grad")
        cols = pl.ds(half * HALF, HALF)

        def slope_step(i, carry):
            rows = pl.ds(pl.multiple_of(i * 16, 16), 16)
            value = part[6, rows, cols].astype(jnp.float32)
            grad = (part[7, rows, cols].astype(jnp.float32) * gelu_slope(value)).astype(jnp.bfloat16)
            for b in range(COLS // 2):
                g_own[half * COLS // 2 + b, rows, :] = grad[:, b * BLOCK:(b + 1) * BLOCK]
            return carry

        lax.fori_loop(0, PANEL // 16, slope_step, 0)
        blocks = pl.ds(half * COLS // 2, COLS // 2)
        remote(("g", half), g_own.at[blocks], g_peer.at[blocks], zhp)

    def selected(panel, k, r, rows):
        grad = (g_own, g_peer)[panel]
        return jnp.concatenate([grad[pat_s[k, s, r], rows, :] for s in range(SLOTS)], axis=1)

    def live(k, r):
        lanes = lax.broadcasted_iota(jnp.int32, (BLOCK, SLOTS * BLOCK), 1)
        return lanes < pat_s[k, SLOTS, r] * BLOCK

    def each_row(body):
        def several(i, carry):
            for v in range(UNROLL):
                r = UNROLL * i + v
                body(r, pl.ds(pl.multiple_of(r * BLOCK, BLOCK), BLOCK))
            return carry

        lax.fori_loop(0, ROWS_DEV // UNROLL, several, 0)

    def partial_half(u, rows, extra):
        panel, k = UNITS[u]
        if panel == 1:
            need(("g", 0), ("g", 1))
        if k == FAR:
            need(("w", FAR), "w far low")

        def body(r, at):
            weights = jnp.where(live(k, r), w_all[k, at, :], jnp.zeros((), jnp.bfloat16))
            total = lax.dot_general(
                selected(panel, k, r, rows), weights, (((1,), (1,)), ((), ())),
                preferred_element_type=jnp.float32,
            )
            if extra:
                total = total + rb1[u, :, at].astype(jnp.float32)
            part[u, rows, at] = total.astype(jnp.bfloat16)

        each_row(body)

    A, B = pl.ds(0, HALF), pl.ds(HALF, HALF)

    def chunk(t):
        return pl.multiple_of(c * 256 + ((y + t) % 4) * 64, 64)

    def first(u):
        rows = rows_of((1 - c) * 256, 256)
        partial_half(u, rows, False)
        remote(("core", u), part.at[u, rows], rb1.at[u], core)

    def second(u):
        need(("core", u))
        partial_half(u, rows_of(c * 256, 256), True)
        if u < 4:
            ring(u)

    def share(u, t, half):
        if u < 4:
            return part.at[u], chunk(t)
        turn = (y + t - zh) % 4
        group = jnp.where(
            half == 0, (turn % 2) * 2 + turn // 2,
            jnp.where(turn % 2 == 0, 2 + turn // 2, 1 - turn // 2),
        )
        step = (group - x) % 4
        index = jnp.where(step == 2, FAR, jnp.where(step == 3, LEFT, step))
        return part.at[4 + index], pl.multiple_of(c * 256 + (u - 4) * 64, 64)

    def share_at(u, t, half):
        ref, row = share(u, t, half)
        return ref.at[pl.ds(row, 64), pl.ds(pl.multiple_of(half * HALF, 128), HALF)]

    def ring(u):
        remote(("r0", u), share_at(u, 2, 0), r2.at[u, 0], yr)
        remote(("r1", u), share_at(u, 2, 1), r2.at[u, 1], yl)
        remote(("r2", u), share_at(u, 1, 1), r2.at[u, 2], yr)
        remote(("r3", u), share_at(u, 3, 0), r2.at[u, 3], yl)

    def step_right(u):
        need(("r0", u))
        ref, row = share(u, 1, 0)
        add_rows(ref, row, A, [(r2.at[u, 0], 0, every)], 64)
        remote(("r4", u), share_at(u, 1, 0), r2.at[u, 4], yr)

    def step_left(u):
        need(("r1", u))
        ref, row = share(u, 3, 1)
        add_rows(ref, row, B, [(r2.at[u, 1], 0, every)], 64)
        remote(("r5", u), share_at(u, 3, 1), r2.at[u, 5], yl)

    finals = []
    crossing = {}
    odd = (y - zh) % 2
    kept = (odd + zl) % 2

    def end_ring(u):
        need(("r3", u), ("r4", u))
        ref, row = share(u, 0, 0)
        add_rows(ref, row, A, [(r2.at[u, 3], 0, every), (r2.at[u, 4], 0, every)], 64)
        need(("r2", u), ("r5", u))
        ref, row = share(u, 0, 1)
        add_rows(ref, row, B, [(r2.at[u, 2], 0, every), (r2.at[u, 5], 0, every)], 64)
        if u >= 4:
            remote(("zl", u), share_at(u, 0, 1 - kept), rb3.at[u, :, A], zlp)
            return
        stays = xg[UNITS[u][1]] // 2 == zl
        i = count["remote"]
        count["remote"] += 1
        cp = pltpu.make_async_remote_copy(
            src_ref=part.at[u, pl.ds(chunk(0), 64)], dst_ref=rb3.at[u],
            send_sem=send.at[i], recv_sem=recv.at[i], device_id=zlp, device_id_type=MESH,
        )

        @pl.when(jnp.logical_not(stays))
        def _():
            cp.start()

        finals.append((cp, jnp.logical_not(stays)))
        crossing[u] = cp, stays


    def to_owner(u):
        panel, k = UNITS[u]
        if panel == 1:
            need(("zl", u))
            ref, row = share(u, 0, kept)
            cols = pl.ds(pl.multiple_of(kept * HALF, 128), HALF)
            add_rows(ref, row, cols, [(rb3.at[u], 0, A)], 64)
            remote(("hop", u), share_at(u, 0, kept), rb4.at[u - 4], zhp)
            return
        cp3, stays = crossing[u]

        @pl.when(stays)
        def _():
            cp3.wait_recv()
            add_rows(part.at[u], chunk(0), every, [(rb3.at[u], 0, every)], 64)

        for j, cols in enumerate((A, B)):
            owner = dev(x, zh, zl, (xg[k] % 2) * 2 + zh, j)
            src = part.at[u, pl.ds(chunk(0), 64), cols]
            dst = gi_ref.at[pl.ds(chunk(0), 64)]
            i = count["remote"]
            count["remote"] += 1
            cp = pltpu.make_async_remote_copy(
                src_ref=src, dst_ref=dst, send_sem=send.at[i], recv_sem=local.at[0],
                device_id=owner, device_id_type=MESH,
            )
            here = jnp.logical_and(owner[1] == h, stays)
            away = jnp.logical_and(owner[1] != h, stays)
            stay = pltpu.make_async_copy(src, dst, local.at[0])

            @pl.when(here)
            def _():
                stay.start()

            @pl.when(away)
            def _():
                cp.start()

            finals.append((cp, away))

    def deliver(u):
        need(("hop", u))
        away_y = (1 - odd) * (1 - 2 * kept)
        src, dst = rb4.at[u - 4], gi_ref.at[rows_of(c * 256 + (u - 4) * 64, 64)]
        i = count["remote"]
        count["remote"] += 1
        cp = pltpu.make_async_remote_copy(
            src_ref=src, dst_ref=dst, send_sem=send.at[i], recv_sem=local.at[0],
            device_id=dev(x, zh, zl, (y + 4 + away_y) % 4, 1 - kept), device_id_type=MESH,
        )
        stay = pltpu.make_async_copy(src, dst, local.at[0])
        moves = jnp.logical_not(stay_put)

        @pl.when(stay_put)
        def _():
            stay.start()

        @pl.when(moves)
        def _():
            cp.start()

        finals.append((cp, moves))

    def spread(k):
        need(("t0", k))
        at = tp_ref.at[k, pl.ds(piece, 64)]
        remote(("t1r", k), at, at, yr)
        remote(("t1l", k), at, at, yl)

    def forward_right(k):
        need(("t1r", k))
        at = tp_ref.at[k, rows_of(chunk(3), 32)]
        remote(("t2r", k), at, at, yr)

    def forward_left(k):
        need(("t1l", k))
        at = tp_ref.at[k, rows_of(chunk(1) + 32, 32)]
        remote(("t2l", k), at, at, yl)

    def tok_core(k):
        need(("t2r", k), ("t2l", k))
        at = tp_ref.at[k, rows_of(c * 256, 256)]
        remote(("t3", k), at, at, core)

    def load_own(k):
        near(("lo", k), tokens.at[:, group_cols(k, zh)], tok_s.at[k])

    def load_peer(k):
        need(("t3", k))
        near(("lp", k), tp_ref.at[k], tok_s.at[k])

    def weight_term(k, panel):
        def body(r, at):
            total = lax.dot_general(
                tok_s[k, :, at], selected(panel, k, r, every), (((0,), (0,)), ((), ())),
                preferred_element_type=jnp.float32,
            )
            total = jnp.where(live(k, r), total, 0.0)
            if panel == 1:
                total = total + dw[k, at, :].astype(jnp.float32)
            dw[k, at, :] = total.astype(jnp.bfloat16)

        each_row(body)

    def term_own(k):
        need(("lo", k))
        weight_term(k, 0)

    def term_peer(k):
        need(("lp", k), ("g", 0), ("g", 1))
        weight_term(k, 1)
        if k == FAR:
            remote("d1r", dw.at[FAR, top], dx.at[0], xr)
            remote("d1l", dw.at[FAR, low], dx.at[1], xl)
        if k == RIGHT:
            remote("dr", dw.at[RIGHT, low], dx.at[2], xr)
        if k == LEFT:
            remote("dl", dw.at[LEFT, top], dx.at[3], xl)

    def pass_right():
        need("d1r")
        add_rows(dw.at[RIGHT], 0, every, [(dx.at[0], 0, every)], HALF)
        remote("d2r", dw.at[RIGHT, top], dx.at[4], xr)

    def pass_left():
        need("d1l")
        add_rows(dw.at[LEFT], HALF, every, [(dx.at[1], 0, every)], HALF)
        remote("d2l", dw.at[LEFT, low], dx.at[5], xl)

    def finish(row, first_, second_):
        def body(i, carry):
            here = pl.ds(pl.multiple_of(row + i * 32, 32), 32)
            there = pl.ds(pl.multiple_of(i * 32, 32), 32)
            total = dw[OWN, here, :].astype(jnp.float32) + dx[first_, there, :].astype(jnp.float32)
            total = total + dx[second_, there, :].astype(jnp.float32)
            gw_ref[here, :] = total.astype(jnp.bfloat16)
            return carry

        lax.fori_loop(0, HALF // 32, body, 0)

    start_patterns()
    start_weights()
    tok0(FAR)
    tok0(RIGHT)
    tok0(LEFT)
    tok0(OWN)
    load_own(FAR)
    load_own(RIGHT)
    load_own(LEFT)
    load_own(OWN)
    gelu(0)
    gelu(1)
    patterns()
    first(0)
    spread(FAR)
    term_own(FAR)
    term_own(RIGHT)
    term_own(LEFT)
    spread(RIGHT)
    second(0)
    term_own(OWN)
    forward_right(FAR)
    forward_left(FAR)
    spread(LEFT)
    forward_right(RIGHT)
    forward_left(RIGHT)
    spread(OWN)
    step_right(0)
    step_left(0)
    tok_core(FAR)
    load_peer(FAR)
    forward_right(LEFT)
    forward_left(LEFT)
    tok_core(RIGHT)
    load_peer(RIGHT)
    forward_weights()
    forward_right(OWN)
    forward_left(OWN)
    first(1)
    end_ring(0)
    tok_core(LEFT)
    second(1)
    tok_core(OWN)
    first(2)
    load_peer(LEFT)
    load_peer(OWN)
    step_right(1)
    step_left(1)
    second(2)
    end_ring(1)
    step_right(2)
    step_left(2)
    term_peer(FAR)
    term_peer(RIGHT)
    first(3)
    end_ring(2)
    first(4)
    second(3)
    first(5)
    first(6)
    second(4)
    first(7)
    second(5)
    second(6)
    step_right(3)
    step_left(3)
    second(7)
    ring(4)
    ring(5)
    term_peer(LEFT)
    step_right(4)
    step_left(4)
    ring(6)
    pass_right()
    pass_left()
    step_right(5)
    step_left(5)
    ring(7)
    term_peer(OWN)
    end_ring(3)
    end_ring(4)
    step_right(6)
    step_left(6)
    end_ring(5)
    to_owner(4)
    step_right(7)
    step_left(7)
    to_owner(0)
    to_owner(1)
    end_ring(6)
    to_owner(5)
    deliver(4)
    to_owner(2)
    to_owner(3)
    end_ring(7)
    to_owner(6)
    deliver(5)
    to_owner(7)
    deliver(6)
    deliver(7)
    need("dl", "d2r")
    finish(0, 3, 4)
    need("dr", "d2l")
    finish(HALF, 2, 5)
    need(*moving)
    if finals:
        pltpu.make_async_copy(gi_ref, gi_ref, local.at[0]).wait()

    for cp in sends:
        cp.wait_send()
    for cp, started in finals:

        @pl.when(started)
        def _():
            cp.wait_send()


N_REMOTE = 144
N_LOCAL = 24


def per_device(tokens, preact, grad_hidden, w_packed, block_cols, block_counts):
    any_space = pl.BlockSpec(memory_space=pl.ANY)
    vmem = pl.BlockSpec(memory_space=pltpu.VMEM)
    bf16 = jnp.bfloat16
    grad_input, grad_weight, _ = pl.pallas_call(
        kernel,
        out_shape=(
            jax.ShapeDtypeStruct((PANEL, HALF), bf16),
            jax.ShapeDtypeStruct((WIDE, SLOTS * BLOCK), bf16),
            jax.ShapeDtypeStruct((4, PANEL, WIDE), bf16),
        ),
        in_specs=[vmem] * 2 + [any_space] * 4,
        out_specs=(any_space, vmem, any_space),
        scratch_shapes=[
            pltpu.VMEM((8, BLOCK), jnp.int32),
            pltpu.VMEM((3, 8, BLOCK), jnp.int32),
            pltpu.SMEM((4, 8, BLOCK), jnp.int32),
            pltpu.VMEM((4, WIDE, SLOTS * BLOCK), bf16),
            pltpu.VMEM((COLS, PANEL, BLOCK), bf16),
            pltpu.VMEM((COLS, PANEL, BLOCK), bf16),
            pltpu.VMEM((4, PANEL, WIDE), bf16),
            pltpu.VMEM((8, PANEL, WIDE), bf16),
            pltpu.VMEM((8, 256, WIDE), bf16),
            pltpu.VMEM((8, 6, 64, HALF), bf16),
            pltpu.VMEM((8, 64, WIDE), bf16),
            pltpu.VMEM((4, 64, HALF), bf16),
            pltpu.VMEM((4, WIDE, SLOTS * BLOCK), bf16),
            pltpu.VMEM((6, HALF, SLOTS * BLOCK), bf16),
            pltpu.SemaphoreType.DMA((N_REMOTE,)),
            pltpu.SemaphoreType.DMA((N_REMOTE,)),
            pltpu.SemaphoreType.DMA((N_LOCAL,)),
        ],
        compiler_params=pltpu.CompilerParams(
            collective_id=0, has_side_effects=True, vmem_limit_bytes=60 << 20
        ),
        name="ffn_backward",
    )(block_cols.T, block_counts.T, tokens, preact, grad_hidden, w_packed)
    return grad_input, grad_weight


def solution(mesh):
    placed = (
        P("feat", None),
        P("feat", "hid"),
        P("feat", "hid"),
        P("feat", "hid"),
        P("feat", "hid"),
        P("feat", "hid"),
    )
    return jax.shard_map(
        per_device,
        mesh=mesh,
        in_specs=placed,
        out_specs=(P("feat", "hid"), P("feat", "hid")),
        check_vma=False,
    )
```

```python
import functools

import jax
import jax.numpy as jnp
from jax import lax
from jax.experimental import pallas as pl
from jax.experimental.pallas import tpu as pltpu
from jax.sharding import PartitionSpec as P

BLOCK = 128
SLOTS = 4
PANEL = 512
ROWS_DEV = 12
WIDE = ROWS_DEV * BLOCK
HALF = WIDE // 2
COLS = 12
CUBIC = 0.044715
ROOT = 0.7978845608028654
MESH = pl.DeviceIdType.MESH
OWN, RIGHT, LEFT, FAR = 0, 1, 2, 3
X_STEP = (0, 1, 3, 2)
UNITS = (
    (0, OWN), (0, RIGHT), (0, LEFT), (0, FAR), (1, OWN), (1, RIGHT), (1, LEFT), (1, FAR),
)
UNROLL = 6


def gelu_slope(values):
    tangent = jnp.tanh(ROOT * (values + CUBIC * values * values * values))
    return 0.5 * (1.0 + tangent) + 0.5 * values * (1.0 - tangent * tangent) * ROOT * (
        1.0 + 3.0 * CUBIC * values * values
    )


def add_rows(dst, dst_row, dst_cols, terms, rows, step=32):
    def body(i, carry):
        off = i * step
        here = (pl.ds(pl.multiple_of(dst_row + off, 16), step), dst_cols)
        total = dst[here].astype(jnp.float32)
        for ref, row, cols in terms:
            total = total + ref[pl.ds(pl.multiple_of(row + off, 16), step), cols].astype(jnp.float32)
        dst[here] = total.astype(jnp.bfloat16)
        return carry

    lax.fori_loop(0, rows // step, body, 0)


def kernel(
    cols_ref, counts_ref, tokens, preact, grad_hidden, w_hbm,
    gi_ref, gw_ref, tp_ref,
    pat_ref, pat_in, pat_s, w_all, g_own, g_peer, tok_s, part, rb1, r2, rb3, rb4, dw, dx,
    send, recv, local,
):
    f, h = lax.axis_index("feat"), lax.axis_index("hid")
    x, zh, zl, y, c = f // 2, f % 2, h // 8, (h // 2) % 4, h % 2

    def dev(x_, zh_, zl_, y_, c_):
        return (x_ * 2 + zh_, zl_ * 8 + y_ * 2 + c_)

    xg = [(x + s) % 4 for s in X_STEP]
    core = dev(x, zh, zl, y, 1 - c)
    xr, xl, xo = dev(xg[RIGHT], zh, zl, y, c), dev(xg[LEFT], zh, zl, y, c), dev(xg[FAR], zh, zl, y, c)
    yr, yl = dev(x, zh, zl, (y + 1) % 4, c), dev(x, zh, zl, (y + 3) % 4, c)
    zlp, zhp = dev(x, zh, 1 - zl, y, c), dev(x, 1 - zh, zl, y, c)

    count = {"remote": 0, "local": 1}
    sends = []
    moving = {}

    def remote(name, src, dst, device):
        i = count["remote"]
        count["remote"] += 1
        cp = pltpu.make_async_remote_copy(
            src_ref=src, dst_ref=dst, send_sem=send.at[i], recv_sem=recv.at[i],
            device_id=device, device_id_type=MESH,
        )
        cp.start()
        sends.append(cp)
        moving[name] = cp.wait_recv

    def near(name, src, dst):
        i = count["local"]
        count["local"] += 1
        cp = pltpu.make_async_copy(src, dst, local.at[i])
        cp.start()
        moving[name] = cp.wait

    def need(*names):
        for name in names:
            wait = moving.get(name)
            if wait is not None:
                wait()
            moving[name] = None

    near("preact", preact, part.at[6])
    near("grad", grad_hidden, part.at[7])
    near(("w", OWN), w_hbm, w_all.at[OWN])
    pat_ref[...] = jnp.zeros_like(pat_ref)
    pat_ref[:SLOTS, :ROWS_DEV] = cols_ref[...]
    pat_ref[SLOTS:SLOTS + 1, :ROWS_DEV] = counts_ref[...]
    near(("pat", OWN), pat_ref, pat_s.at[OWN])

    barrier = pltpu.get_barrier_semaphore()

    def greet(device):
        pl.semaphore_signal(barrier, inc=1, device_id=device, device_id_type=MESH)

    for device in (core, xr, xl, xo, yr, yl, zlp, zhp):
        greet(device)
    mine = (y % 2) == zh
    side = jnp.where(c == zl, y, (y + 3 + 2 * zl) % 4)
    for t in range(4):
        for other_c in range(2):
            other_y = (y + t) % 4
            if t == 0:
                other_y = jnp.where(mine, y, side)
                sends_here = jnp.logical_not(jnp.logical_and(other_y == y, c == other_c))
            else:
                sends_here = mine

            @pl.when(sends_here)
            def _():
                greet(dev(x, zh, zl, other_y, other_c))

    stay_put = jnp.logical_and(jnp.logical_not(mine), c == zl)
    pl.semaphore_wait(barrier, 13 - mine.astype(jnp.int32) - stay_put.astype(jnp.int32))

    def start_patterns():
        for i, (k, device) in enumerate(((LEFT, xr), (RIGHT, xl), (FAR, xo))):
            remote(("pat", k), pat_ref, pat_in.at[i], device)

    def start_weights():
        remote(("w", LEFT), w_hbm, w_all.at[LEFT], xr)
        remote(("w", RIGHT), w_hbm, w_all.at[RIGHT], xl)

    def patterns():
        for i, k in enumerate((LEFT, RIGHT, FAR)):
            need(("pat", k))
            near(("pat in", k), pat_in.at[i], pat_s.at[k])
        for k in (LEFT, RIGHT, FAR):
            need(("pat in", k))
        need(("w", OWN), ("pat", OWN))

    top, low = pl.ds(0, HALF), pl.ds(HALF, HALF)

    def forward_weights():
        need(("w", LEFT), ("w", RIGHT))
        remote(("w", FAR), w_all.at[LEFT, top], w_all.at[FAR, top], xr)
        remote("w far low", w_all.at[RIGHT, low], w_all.at[FAR, low], xl)

    piece = pl.multiple_of(c * 256 + y * 64, 64)
    every = slice(None)

    def rows_of(at, n):
        return pl.ds(pl.multiple_of(at, 16), n)

    def group_cols(k, zh_):
        return pl.ds(pl.multiple_of((2 * xg[k] + zh_) * WIDE, 128), WIDE)

    def tok0(k):
        rows = pl.ds(piece, 64)
        remote(("t0", k), tokens.at[rows, group_cols(k, 1 - zh)], tp_ref.at[k, rows], zhp)

    def gelu(half):
        need("preact", "grad")
        cols = pl.ds(half * HALF, HALF)

        def slope_step(i, carry):
            rows = pl.ds(pl.multiple_of(i * 16, 16), 16)
            value = part[6, rows, cols].astype(jnp.float32)
            grad = (part[7, rows, cols].astype(jnp.float32) * gelu_slope(value)).astype(jnp.bfloat16)
            for b in range(COLS // 2):
                g_own[half * COLS // 2 + b, rows, :] = grad[:, b * BLOCK:(b + 1) * BLOCK]
            return carry

        lax.fori_loop(0, PANEL // 16, slope_step, 0)
        blocks = pl.ds(half * COLS // 2, COLS // 2)
        remote(("g", half), g_own.at[blocks], g_peer.at[blocks], zhp)

    def selected(panel, k, r, rows):
        grad = (g_own, g_peer)[panel]
        return jnp.concatenate([grad[pat_s[k, s, r], rows, :] for s in range(SLOTS)], axis=1)

    def live(k, r):
        lanes = lax.broadcasted_iota(jnp.int32, (BLOCK, SLOTS * BLOCK), 1)
        return lanes < pat_s[k, SLOTS, r] * BLOCK

    def each_row(body):
        def several(i, carry):
            for v in range(UNROLL):
                r = UNROLL * i + v
                body(r, pl.ds(pl.multiple_of(r * BLOCK, BLOCK), BLOCK))
            return carry

        lax.fori_loop(0, ROWS_DEV // UNROLL, several, 0)

    def partial_half(u, rows, extra):
        panel, k = UNITS[u]
        if panel == 1:
            need(("g", 0), ("g", 1))
        if k == FAR:
            need(("w", FAR), "w far low")

        def body(r, at):
            weights = jnp.where(live(k, r), w_all[k, at, :], jnp.zeros((), jnp.bfloat16))
            total = lax.dot_general(
                selected(panel, k, r, rows), weights, (((1,), (1,)), ((), ())),
                preferred_element_type=jnp.float32,
            )
            if extra:
                total = total + rb1[u, :, at].astype(jnp.float32)
            part[u, rows, at] = total.astype(jnp.bfloat16)

        each_row(body)

    A, B = pl.ds(0, HALF), pl.ds(HALF, HALF)

    def chunk(t):
        return pl.multiple_of(c * 256 + ((y + t) % 4) * 64, 64)

    def first(u):
        rows = rows_of((1 - c) * 256, 256)
        partial_half(u, rows, False)
        remote(("core", u), part.at[u, rows], rb1.at[u], core)

    def second(u):
        need(("core", u))
        partial_half(u, rows_of(c * 256, 256), True)
        if u < 4:
            ring(u)

    def share(u, t, half):
        if u < 4:
            return part.at[u], chunk(t)
        turn = (y + t - zh) % 4
        group = jnp.where(
            half == 0, (turn % 2) * 2 + turn // 2,
            jnp.where(turn % 2 == 0, 2 + turn // 2, 1 - turn // 2),
        )
        step = (group - x) % 4
        index = jnp.where(step == 2, FAR, jnp.where(step == 3, LEFT, step))
        return part.at[4 + index], pl.multiple_of(c * 256 + (u - 4) * 64, 64)

    def share_at(u, t, half):
        ref, row = share(u, t, half)
        return ref.at[pl.ds(row, 64), pl.ds(pl.multiple_of(half * HALF, 128), HALF)]

    def ring(u):
        remote(("r0", u), share_at(u, 2, 0), r2.at[u, 0], yr)
        remote(("r1", u), share_at(u, 2, 1), r2.at[u, 1], yl)
        remote(("r2", u), share_at(u, 1, 1), r2.at[u, 2], yr)
        remote(("r3", u), share_at(u, 3, 0), r2.at[u, 3], yl)

    def step_right(u):
        need(("r0", u))
        ref, row = share(u, 1, 0)
        add_rows(ref, row, A, [(r2.at[u, 0], 0, every)], 64)
        remote(("r4", u), share_at(u, 1, 0), r2.at[u, 4], yr)

    def step_left(u):
        need(("r1", u))
        ref, row = share(u, 3, 1)
        add_rows(ref, row, B, [(r2.at[u, 1], 0, every)], 64)
        remote(("r5", u), share_at(u, 3, 1), r2.at[u, 5], yl)

    finals = []
    crossing = {}
    odd = (y - zh) % 2
    kept = (odd + zl) % 2

    def end_ring(u):
        need(("r3", u), ("r4", u))
        ref, row = share(u, 0, 0)
        add_rows(ref, row, A, [(r2.at[u, 3], 0, every), (r2.at[u, 4], 0, every)], 64)
        need(("r2", u), ("r5", u))
        ref, row = share(u, 0, 1)
        add_rows(ref, row, B, [(r2.at[u, 2], 0, every), (r2.at[u, 5], 0, every)], 64)
        if u >= 4:
            remote(("zl", u), share_at(u, 0, 1 - kept), rb3.at[u, :, A], zlp)
            return
        stays = xg[UNITS[u][1]] // 2 == zl
        i = count["remote"]
        count["remote"] += 1
        cp = pltpu.make_async_remote_copy(
            src_ref=part.at[u, pl.ds(chunk(0), 64)], dst_ref=rb3.at[u],
            send_sem=send.at[i], recv_sem=recv.at[i], device_id=zlp, device_id_type=MESH,
        )

        @pl.when(jnp.logical_not(stays))
        def _():
            cp.start()

        finals.append((cp, jnp.logical_not(stays)))
        crossing[u] = cp, stays


    def to_owner(u):
        panel, k = UNITS[u]
        if panel == 1:
            need(("zl", u))
            ref, row = share(u, 0, kept)
            cols = pl.ds(pl.multiple_of(kept * HALF, 128), HALF)
            add_rows(ref, row, cols, [(rb3.at[u], 0, A)], 64)
            remote(("hop", u), share_at(u, 0, kept), rb4.at[u - 4], zhp)
            return
        cp3, stays = crossing[u]

        @pl.when(stays)
        def _():
            cp3.wait_recv()
            add_rows(part.at[u], chunk(0), every, [(rb3.at[u], 0, every)], 64)

        for j, cols in enumerate((A, B)):
            owner = dev(x, zh, zl, (xg[k] % 2) * 2 + zh, j)
            src = part.at[u, pl.ds(chunk(0), 64), cols]
            dst = gi_ref.at[pl.ds(chunk(0), 64)]
            i = count["remote"]
            count["remote"] += 1
            cp = pltpu.make_async_remote_copy(
                src_ref=src, dst_ref=dst, send_sem=send.at[i], recv_sem=local.at[0],
                device_id=owner, device_id_type=MESH,
            )
            here = jnp.logical_and(owner[1] == h, stays)
            away = jnp.logical_and(owner[1] != h, stays)
            stay = pltpu.make_async_copy(src, dst, local.at[0])

            @pl.when(here)
            def _():
                stay.start()

            @pl.when(away)
            def _():
                cp.start()

            finals.append((cp, away))

    def deliver(u):
        need(("hop", u))
        away_y = (1 - odd) * (1 - 2 * kept)
        src, dst = rb4.at[u - 4], gi_ref.at[rows_of(c * 256 + (u - 4) * 64, 64)]
        i = count["remote"]
        count["remote"] += 1
        cp = pltpu.make_async_remote_copy(
            src_ref=src, dst_ref=dst, send_sem=send.at[i], recv_sem=local.at[0],
            device_id=dev(x, zh, zl, (y + 4 + away_y) % 4, 1 - kept), device_id_type=MESH,
        )
        stay = pltpu.make_async_copy(src, dst, local.at[0])
        moves = jnp.logical_not(stay_put)

        @pl.when(stay_put)
        def _():
            stay.start()

        @pl.when(moves)
        def _():
            cp.start()

        finals.append((cp, moves))

    def spread(k):
        need(("t0", k))
        at = tp_ref.at[k, pl.ds(piece, 64)]
        remote(("t1r", k), at, at, yr)
        remote(("t1l", k), at, at, yl)

    def forward_right(k):
        need(("t1r", k))
        at = tp_ref.at[k, rows_of(chunk(3), 32)]
        remote(("t2r", k), at, at, yr)

    def forward_left(k):
        need(("t1l", k))
        at = tp_ref.at[k, rows_of(chunk(1) + 32, 32)]
        remote(("t2l", k), at, at, yl)

    def tok_core(k):
        need(("t2r", k), ("t2l", k))
        at = tp_ref.at[k, rows_of(c * 256, 256)]
        remote(("t3", k), at, at, core)

    def load_own(k):
        near(("lo", k), tokens.at[:, group_cols(k, zh)], tok_s.at[k])

    def load_peer(k):
        need(("t3", k))
        near(("lp", k), tp_ref.at[k], tok_s.at[k])

    def weight_term(k, panel):
        def body(r, at):
            total = lax.dot_general(
                tok_s[k, :, at], selected(panel, k, r, every), (((0,), (0,)), ((), ())),
                preferred_element_type=jnp.float32,
            )
            total = jnp.where(live(k, r), total, 0.0)
            if panel == 1:
                total = total + dw[k, at, :].astype(jnp.float32)
            dw[k, at, :] = total.astype(jnp.bfloat16)

        each_row(body)

    def term_own(k):
        need(("lo", k))
        weight_term(k, 0)

    def term_peer(k):
        need(("lp", k), ("g", 0), ("g", 1))
        weight_term(k, 1)
        if k == FAR:
            remote("d1r", dw.at[FAR, top], dx.at[0], xr)
            remote("d1l", dw.at[FAR, low], dx.at[1], xl)
        if k == RIGHT:
            remote("dr", dw.at[RIGHT, low], dx.at[2], xr)
        if k == LEFT:
            remote("dl", dw.at[LEFT, top], dx.at[3], xl)

    def pass_right():
        need("d1r")
        add_rows(dw.at[RIGHT], 0, every, [(dx.at[0], 0, every)], HALF)
        remote("d2r", dw.at[RIGHT, top], dx.at[4], xr)

    def pass_left():
        need("d1l")
        add_rows(dw.at[LEFT], HALF, every, [(dx.at[1], 0, every)], HALF)
        remote("d2l", dw.at[LEFT, low], dx.at[5], xl)

    def finish(row, first_, second_):
        def body(i, carry):
            here = pl.ds(pl.multiple_of(row + i * 32, 32), 32)
            there = pl.ds(pl.multiple_of(i * 32, 32), 32)
            total = dw[OWN, here, :].astype(jnp.float32) + dx[first_, there, :].astype(jnp.float32)
            total = total + dx[second_, there, :].astype(jnp.float32)
            dw[OWN, here, :] = total.astype(jnp.bfloat16)
            return carry

        lax.fori_loop(0, HALF // 32, body, 0)
        near(("gw", row), dw.at[OWN, pl.ds(row, HALF)], gw_ref.at[pl.ds(row, HALF)])

    start_patterns()
    start_weights()
    tok0(FAR)
    tok0(RIGHT)
    tok0(LEFT)
    tok0(OWN)
    load_own(FAR)
    load_own(RIGHT)
    load_own(LEFT)
    load_own(OWN)
    gelu(0)
    gelu(1)
    patterns()
    first(0)
    spread(FAR)
    term_own(FAR)
    term_own(RIGHT)
    term_own(LEFT)
    spread(RIGHT)
    second(0)
    term_own(OWN)
    forward_right(FAR)
    forward_left(FAR)
    spread(LEFT)
    forward_right(RIGHT)
    forward_left(RIGHT)
    spread(OWN)
    step_right(0)
    step_left(0)
    tok_core(FAR)
    load_peer(FAR)
    forward_right(LEFT)
    forward_left(LEFT)
    tok_core(RIGHT)
    load_peer(RIGHT)
    forward_weights()
    forward_right(OWN)
    forward_left(OWN)
    first(1)
    end_ring(0)
    tok_core(LEFT)
    second(1)
    tok_core(OWN)
    first(2)
    load_peer(LEFT)
    load_peer(OWN)
    step_right(1)
    step_left(1)
    second(2)
    end_ring(1)
    step_right(2)
    step_left(2)
    term_peer(FAR)
    term_peer(RIGHT)
    first(3)
    end_ring(2)
    first(4)
    second(3)
    first(5)
    first(6)
    second(4)
    first(7)
    second(5)
    second(6)
    step_right(3)
    step_left(3)
    second(7)
    ring(4)
    ring(5)
    term_peer(LEFT)
    step_right(4)
    step_left(4)
    ring(6)
    pass_right()
    pass_left()
    step_right(5)
    step_left(5)
    ring(7)
    term_peer(OWN)
    end_ring(3)
    end_ring(4)
    step_right(6)
    step_left(6)
    end_ring(5)
    to_owner(4)
    step_right(7)
    step_left(7)
    to_owner(0)
    to_owner(1)
    end_ring(6)
    to_owner(5)
    deliver(4)
    to_owner(2)
    to_owner(3)
    end_ring(7)
    to_owner(6)
    deliver(5)
    to_owner(7)
    deliver(6)
    deliver(7)
    need("dl", "d2r")
    finish(0, 3, 4)
    need("dr", "d2l")
    finish(HALF, 2, 5)
    need(*moving)
    if finals:
        pltpu.make_async_copy(gi_ref, gi_ref, local.at[0]).wait()

    for cp in sends:
        cp.wait_send()
    for cp, started in finals:

        @pl.when(started)
        def _():
            cp.wait_send()


N_REMOTE = 144
N_LOCAL = 24


def per_device(tokens, preact, grad_hidden, w_packed, block_cols, block_counts):
    any_space = pl.BlockSpec(memory_space=pl.ANY)
    vmem = pl.BlockSpec(memory_space=pltpu.VMEM)
    bf16 = jnp.bfloat16
    grad_input, grad_weight, _ = pl.pallas_call(
        kernel,
        out_shape=(
            jax.ShapeDtypeStruct((PANEL, HALF), bf16),
            jax.ShapeDtypeStruct((WIDE, SLOTS * BLOCK), bf16),
            jax.ShapeDtypeStruct((4, PANEL, WIDE), bf16),
        ),
        in_specs=[vmem] * 2 + [any_space] * 4,
        out_specs=(any_space,) * 3,
        scratch_shapes=[
            pltpu.VMEM((8, BLOCK), jnp.int32),
            pltpu.VMEM((3, 8, BLOCK), jnp.int32),
            pltpu.SMEM((4, 8, BLOCK), jnp.int32),
            pltpu.VMEM((4, WIDE, SLOTS * BLOCK), bf16),
            pltpu.VMEM((COLS, PANEL, BLOCK), bf16),
            pltpu.VMEM((COLS, PANEL, BLOCK), bf16),
            pltpu.VMEM((4, PANEL, WIDE), bf16),
            pltpu.VMEM((8, PANEL, WIDE), bf16),
            pltpu.VMEM((8, 256, WIDE), bf16),
            pltpu.VMEM((8, 6, 64, HALF), bf16),
            pltpu.VMEM((8, 64, WIDE), bf16),
            pltpu.VMEM((4, 64, HALF), bf16),
            pltpu.VMEM((4, WIDE, SLOTS * BLOCK), bf16),
            pltpu.VMEM((6, HALF, SLOTS * BLOCK), bf16),
            pltpu.SemaphoreType.DMA((N_REMOTE,)),
            pltpu.SemaphoreType.DMA((N_REMOTE,)),
            pltpu.SemaphoreType.DMA((N_LOCAL,)),
        ],
        compiler_params=pltpu.CompilerParams(
            collective_id=0, has_side_effects=True, vmem_limit_bytes=60 << 20
        ),
        name="ffn_backward",
    )(block_cols.T, block_counts.T, tokens, preact, grad_hidden, w_packed)
    return grad_input, grad_weight


def solution(mesh):
    placed = (
        P("feat", None),
        P("feat", "hid"),
        P("feat", "hid"),
        P("feat", "hid"),
        P("feat", "hid"),
        P("feat", "hid"),
    )
    return jax.shard_map(
        per_device,
        mesh=mesh,
        in_specs=placed,
        out_specs=(P("feat", "hid"), P("feat", "hid")),
        check_vma=False,
    )
```
